512 devices in a mesh: segment: 8 (over z), dom: 64 (over x, y, core).
Axes of the slice: x: 4, y: 8, z: 8, core: 2. Of those that a mesh axis runs over, the one named last changes fastest.
Arguments:
- features: bfloat16 [32768, 512], P('dom'), may hold values from -6 to 6
- history: bfloat16 [24, 32768, 512], P('segment', 'dom'), may hold values from 0 to 1.5
- weights: bfloat16 [24, 512, 512], P('segment'), may hold values from -0.25 to 0.25
- send_rows: int32 [64, 64, 16], P('dom'), may hold values from 0 to 511
- send_count: int32 [64, 64], P('dom'), may hold values from 0 to 16, as said below
- adj_src: int32 [256, 6], P('dom'), may hold values from 0 to 8, as said below
- adj_blocks: bfloat16 [256, 6, 128, 128], P('dom'), as said below
Outputs:
- fresh: bfloat16 [8, 32768, 512], P('segment', 'dom')
The draws below stay inside these ranges and needn't reach their ends.
Inputs may be any that keep to these rules, and one draw needn't show every extreme that they name: `send_count`: every sender has one receiver with exactly 16 live slots, and every receiver one such sender. `adj_src`: the entries of a row are distinct; the first one of every destination tile is 0, its own local tile. `adj_blocks`: non-negative.
All inputs are finite; a program needn't handle non-finite values.
Results may differ from the reference program's by a relative error of at most 0.0033.
Values may be sent and summed in bfloat16 or wider, within the bound.
No kernel may reach another device: no remote copies, remote signals or barrier semaphores. Data moves between devices by JAX's collectives and lax.ppermute only.
A program may use at most 128 MiB of HBM per device.

```python
import jax
import jax.numpy as jnp
from jax import lax

D = 512
TILE = 128
LPS = 3
MICRO = 4
MB_TILES = 1
HALO_ROWS = 1024
SRC_PER_TILE = 6
NNZ = 16
NPART = 64
LAYERS = 24
ROWS_DEV = 512
NODES = 32768
CAP = 16
SRC_TILES = 9
DEST_TILES = 256


def draw_send_count(key, part):
    key = jax.random.fold_in(key, 5)
    key_list = jax.random.split(key, 4)
    busy_dest = jax.random.randint(key_list[0], (NPART,), 0, 4) == 0
    high_load = jax.random.randint(key_list[1], (NPART, NPART), CAP // 2, CAP + 1)
    light_load = jax.random.randint(key_list[2], (NPART, NPART), 0, CAP // 2 + 1)
    counts = jnp.where(busy_dest[None, :], high_load, light_load)
    pairing = jax.random.permutation(key_list[3], NPART)
    full_pair = pairing[:, None] == jnp.arange(NPART)[None, :]
    return jnp.where(full_pair, CAP, counts).astype(jnp.int32)


def draw_adj_src(key, part):
    key = jax.random.fold_in(key, 7)
    scores = jax.random.randint(key, (DEST_TILES, SRC_TILES), 0, 2 ** 20) * SRC_TILES + jnp.arange(SRC_TILES)[None, :]
    own_tile = jnp.arange(DEST_TILES) % MB_TILES
    scores = jnp.where(jnp.arange(SRC_TILES)[None, :] == own_tile[:, None], -1, scores)
    return jnp.argsort(scores, axis=1)[:, :SRC_PER_TILE].astype(jnp.int32)


def draw_adj_blocks(key, part):
    key = jax.random.fold_in(key, 9)
    key_list = jax.random.split(key, 3)
    shape_all = (DEST_TILES, SRC_PER_TILE, TILE, TILE)
    keep_edge = jax.random.uniform(key_list[0], shape_all) < NNZ / (SRC_PER_TILE * TILE)
    strength = jax.random.uniform(key_list[1], shape_all, minval=0.5, maxval=1.5)
    self_weight = jax.random.uniform(key_list[2], (DEST_TILES, TILE), minval=0.35, maxval=0.65)
    eye_tile = jnp.arange(TILE)[:, None] == jnp.arange(TILE)[None, :]
    first_slot = (jnp.arange(SRC_PER_TILE) == 0)[None, :, None, None]
    diagonal_mask = first_slot & eye_tile[None, None, :, :]
    off_diagonal = jnp.where(keep_edge, strength / NNZ, 0.0)
    off_diagonal = jnp.where(diagonal_mask, 0.0, off_diagonal)
    self_part = jnp.where(diagonal_mask, self_weight[:, None, :, None], 0.0)
    return (off_diagonal + self_part).astype(jnp.float32).astype(jnp.bfloat16)


def with_ends(drawn, own_key, low, top_value):
    spot = [jax.random.randint(jax.random.fold_in(own_key, axis), (), 0, length) for axis, length in enumerate(drawn.shape)]
    main_axis = drawn.shape.index(max(drawn.shape))
    beside = spot[:main_axis] + [(spot[main_axis] + 1) % drawn.shape[main_axis]] + spot[main_axis + 1:]
    return drawn.at[tuple(spot)].set(low).at[tuple(beside)].set(top_value)


def shard_levels(rng, extent, cuts, low, high):
    def one(axis_at, shards_of):
        steps = jax.random.uniform(jax.random.fold_in(jax.random.fold_in(rng, 6), axis_at), (shards_of,), jnp.float32, low / len(cuts), high / len(cuts))
        return jnp.repeat(jnp.exp(steps), extent[axis_at] // shards_of).reshape((-1,) + (1,) * (len(extent) - axis_at - 1))

    loudness = one(*cuts[0])
    for cut in cuts[1:]:
        loudness = loudness * one(*cut)
    return loudness


def scatter_about(key, extent, width, bound, cuts=(), held_as=jnp.bfloat16):
    array = jax.random.normal(key, extent, jnp.float32) * width
    if len(cuts) > 0:
        array = shard_levels(key, extent, cuts, -0.22, 0.18) * array
    return jnp.clip(array, min=-bound, max=bound).astype(held_as)


def setup_inputs(seed: int = 0) -> dict:
    key_of = jax.random.split(jax.random.key(seed), 8)
    features = scatter_about(key_of[0], (NODES, D), 1.0, 6.0, ((0, 64),))
    history = jnp.clip(1.5 * jax.random.uniform(key_of[1], (LAYERS, NODES, D), jnp.float32) ** shard_levels(key_of[1], (LAYERS, NODES, D), ((0, 8), (1, 64)), -0.2, 0.2), 0.0, 1.5).astype(jnp.bfloat16)
    weights = scatter_about(key_of[2], (LAYERS, D, D), D ** -0.5, 0.25, ((0, 8),))
    send_rows = with_ends(jax.random.randint(key_of[3], (NPART, NPART, CAP), 0, ROWS_DEV), jax.random.fold_in(key_of[3], 1), 0, ROWS_DEV - 1).astype(jnp.int32)
    send_count = draw_send_count(jax.random.fold_in(key_of[7], 71), 0)
    adj_src = draw_adj_src(jax.random.fold_in(key_of[7], 71), 0)
    adj_blocks = draw_adj_blocks(jax.random.fold_in(key_of[7], 71), 0)
    return {"features": features, "history": history, "weights": weights, "send_rows": send_rows, "send_count": send_count, "adj_src": adj_src, "adj_blocks": adj_blocks}


def reference(features, history, weights, send_rows, send_count, adj_src, adj_blocks):
    beta_values = jnp.log1p(1.0 / (jnp.arange(LAYERS, dtype=jnp.float32) + 1.0))
    slot_live = jnp.arange(CAP)[None, None, :] < send_count[:, :, None]
    rows_by_dest = jnp.transpose(send_rows, (1, 0, 2))
    live_by_dest = jnp.transpose(slot_live, (1, 0, 2))
    source_ids = adj_src.reshape(NPART, MICRO, MB_TILES, SRC_PER_TILE)
    block_table = adj_blocks.reshape(NPART, MICRO, MB_TILES, SRC_PER_TILE, TILE, TILE)
    initial = features.reshape(NPART, MICRO, MB_TILES * TILE, D)
    hidden = initial
    outputs = []
    part_range = jnp.arange(NPART)[:, None]
    for layer_pos in range(LAYERS):
        history_now = history[layer_pos].reshape(NPART, ROWS_DEV, D)
        beta = beta_values[layer_pos]
        weight_now = weights[layer_pos]

        def one_partition(operands):
            hidden_part, initial_part, rows_part, live_part, ids_part, blocks_part = operands
            pulled = history_now[part_range, rows_part]
            pulled = jnp.where(live_part[:, :, None], pulled, jnp.zeros((), history_now.dtype))
            halo_tiles = pulled.reshape(HALO_ROWS // TILE, TILE, D)
            local_tiles = hidden_part.reshape(MICRO, MB_TILES, TILE, D)
            sources = jnp.concatenate([local_tiles, jnp.broadcast_to(halo_tiles[None], (MICRO,) + halo_tiles.shape)], axis=1)
            picked = jax.vmap(lambda src_tiles, chosen: src_tiles[chosen])(sources, ids_part)
            summed = jnp.einsum('mtkab,mtkbd->mtad', blocks_part.astype(jnp.float32), picked.astype(jnp.float32))
            summed = summed.reshape(MICRO, MB_TILES * TILE, D)
            support = 0.9 * summed + 0.1 * initial_part.astype(jnp.float32)
            branch = jnp.dot(support.astype(jnp.bfloat16).reshape(-1, D), weight_now, preferred_element_type=jnp.float32)
            branch = branch.reshape(support.shape)
            return jax.nn.relu((1.0 - beta) * support + beta * branch).astype(jnp.bfloat16)

        hidden = lax.map(one_partition, (hidden, initial, rows_by_dest, live_by_dest, source_ids, block_table))
        if (layer_pos + 1) % LPS == 0:
            outputs.append(hidden.reshape(NODES, D))
    return jnp.stack(outputs)
```

```python
import jax
import jax.numpy as jnp
import numpy as np
from jax import lax
from jax.experimental import pallas as pl
from jax.experimental.pallas import tpu as pltpu
from jax.sharding import PartitionSpec as P

MICRO = 4
CORES = 2
BOTH = ("segment", "dom")


def chain_kernel(segments, levels, betas, *refs):
    x_ref, a_ref = refs[:2]
    w_refs = refs[2 : 2 + segments]
    h_refs = refs[2 + segments : 2 + segments * (1 + levels)]
    out_ref, w_buf, h_buf, w_sem, h_sem = refs[2 + segments * (1 + levels) :]
    mine = lax.axis_index("segment")

    def w_copy(j, s):
        return pltpu.make_async_copy(w_refs[j], w_buf.at[s], w_sem.at[s])

    def h_copy(j, i, s):
        return pltpu.make_async_copy(h_refs[i * segments + j], h_buf.at[s, i], h_sem.at[s, i])

    for s in range(segments):
        shard = lax.rem(mine - s + segments, segments)
        for j in range(segments):

            @pl.when(shard == j)
            def _():
                for i in range(levels):
                    h_copy(j, i, s).start()
                w_copy(j, s).start()

    a = a_ref[...]
    x = x_ref[...]
    for s in range(segments):
        w_copy(0, s).wait()
        for i in range(levels):
            h_copy(0, i, s).wait()
            beta = betas[s * levels + i]
            summed = jnp.dot(a, x, preferred_element_type=jnp.float32)
            support = 0.9 * summed + h_buf[s, i].astype(jnp.float32)
            branch = jnp.dot(
                support.astype(jnp.bfloat16), w_buf[s, i], preferred_element_type=jnp.float32
            )
            x = jnp.maximum((1.0 - beta) * support + beta * branch, 0.0).astype(jnp.bfloat16)
        out_ref[s] = x


def chain(x, a, weight_shards, halo_shards):
    segments = len(weight_shards)
    levels, width, _ = weight_shards[0].shape
    rows = x.shape[0]
    order = np.arange(segments * levels, dtype=np.float32)
    betas = [float(b) for b in np.log1p(np.float32(1.0) / (order + np.float32(1.0)))]
    anywhere = pl.BlockSpec(memory_space=pl.ANY)
    vmem = pl.BlockSpec(memory_space=pltpu.VMEM)
    flat_halo = [h for level in halo_shards for h in level]
    return pl.pallas_call(
        lambda *refs: chain_kernel(segments, levels, betas, *refs),
        out_shape=jax.ShapeDtypeStruct((segments, rows, width), jnp.bfloat16),
        in_specs=[vmem, vmem] + [anywhere] * (len(weight_shards) + len(flat_halo)),
        out_specs=vmem,
        scratch_shapes=[
            pltpu.VMEM((segments, levels, width, width), jnp.bfloat16),
            pltpu.VMEM((segments, levels, rows, width), jnp.bfloat16),
            pltpu.SemaphoreType.DMA((segments,)),
            pltpu.SemaphoreType.DMA((segments, levels)),
        ],
        compiler_params=pltpu.CompilerParams(vmem_limit_bytes=32 * 1024 * 1024),
        cost_estimate=pl.CostEstimate(
            flops=2 * segments * levels * rows * width * (width + rows),
            bytes_accessed=2 * segments * levels * width * (width + rows),
            transcendentals=0,
        ),
    )(x, a, *weight_shards, *flat_halo)


def local(features, history, weights, send_rows, send_count, adj_src, adj_blocks):
    rows_dev, width = features.shape
    levels = weights.shape[0]
    tile_rows = adj_blocks.shape[2]
    part_count, slot_count = send_rows.shape[1:]
    halo_rows = part_count * slot_count
    halo_tiles = halo_rows // tile_rows
    segments = lax.axis_size("segment")
    parts = lax.axis_size("dom")
    mine = lax.axis_index("segment")
    core = lax.rem(lax.axis_index("dom"), CORES)

    def owner_index(z, pair):
        return z * parts + pair * CORES + z % CORES

    def along_owners(block, step):
        route = [
            (owner_index(z, pair), owner_index((z + step) % segments, pair))
            for z in range(segments)
            for pair in range(parts // CORES)
        ]
        return lax.ppermute(block, BOTH, route)

    def to_owner(block, step):
        route = [
            (z * parts + d, (z + step) % segments * parts + d)
            for z in range(segments)
            for d in range(parts)
            if (z + step) % segments % CORES == d % CORES
        ]
        return lax.ppermute(block, BOTH, route)

    def from_owner(block, step):
        route = [
            (z * parts + d, (z + step) % segments * parts + d)
            for z in range(segments)
            for d in range(parts)
            if z % CORES == d % CORES
        ]
        return lax.ppermute(block, BOTH, route)

    live = jnp.arange(slot_count)[None, :] < send_count[0][:, None]
    wanted = jnp.where(live, send_rows[0], -1).reshape(halo_rows)
    pick = (wanted[:, None] == jnp.arange(rows_dev)[None, :]).astype(jnp.bfloat16)
    arrived = []
    for i in range(levels):
        outgoing = jnp.dot(pick, history[i], preferred_element_type=jnp.float32)
        outgoing = outgoing.astype(jnp.bfloat16).reshape(part_count, slot_count, width)
        arrived.append(
            lax.all_to_all(outgoing, "dom", split_axis=0, concat_axis=0, tiled=True)
        )

    shards = [weights] + [None] * (segments - 1)
    for k in range(1, segments // 2 + 1):
        shards[k] = along_owners(shards[k - 1], 1)
    for k in range(1, segments - segments // 2):
        shards[segments - k] = along_owners(shards[(segments - k + 1) % segments], -1)

    spread = sum(
        jnp.where(
            (adj_src[:, k, None] - 1 == jnp.arange(halo_tiles)[None, :])[:, None, :, None],
            adj_blocks[:, k, :, None, :],
            jnp.zeros((), jnp.bfloat16),
        )
        for k in range(1, adj_src.shape[1])
    ).reshape(rows_dev, halo_rows)

    halo_shards = []
    for i in range(levels):
        summed = jnp.dot(
            spread, arrived[i].reshape(halo_rows, width), preferred_element_type=jnp.float32
        )
        part = (0.9 * summed + 0.1 * features.astype(jnp.float32)).astype(jnp.bfloat16)
        part = part.reshape(MICRO, tile_rows, width)
        level = []
        for k in range(segments):
            target = lax.rem(mine + k, segments)
            block = lax.dynamic_index_in_dim(part, target // CORES, 0, keepdims=False)
            level.append(block if k == 0 else to_owner(block, k))
        halo_shards.append(level)

    tile = mine // CORES
    x = lax.dynamic_slice_in_dim(features, tile * tile_rows, tile_rows, 0)
    a = lax.dynamic_index_in_dim(adj_blocks[:, 0], tile, 0, keepdims=False)
    done = chain(x, a, shards, halo_shards)

    odd = lax.rem(mine + core, CORES)
    got = []
    for k in range(segments):
        target = lax.rem(mine + k, segments)
        block = lax.dynamic_index_in_dim(done, target, 0, keepdims=False)
        got.append(block if k == 0 else from_owner(block, k))
    pairs = jnp.stack(
        [jnp.where(odd == 0, got[k], got[k + 1]) for k in range(0, segments, CORES)]
    )
    last = (mine - core - odd + segments) // CORES
    tiles = [
        lax.dynamic_index_in_dim(pairs, lax.rem(last - m + MICRO, MICRO), 0, keepdims=False)
        for m in range(MICRO)
    ]
    return jnp.concatenate(tiles, axis=0)[None]


def solution(mesh):
    placed = (
        P("dom", None),
        P("segment", "dom", None),
        P("segment", None, None),
        P("dom", None, None),
        P("dom", None),
        P("dom", None),
        P("dom", None, None, None),
    )
    return jax.shard_map(
        local, mesh=mesh, in_specs=placed, out_specs=P("segment", "dom", None), check_vma=False
    )
```

```python
import jax
import jax.numpy as jnp
import numpy as np
from jax import lax
from jax.experimental import pallas as pl
from jax.experimental.pallas import tpu as pltpu
from jax.sharding import Mesh, PartitionSpec as P

HALVES = 2
STAGES = 4
CORES = 2
SEGMENT = ("half", "stage")
DOM = ("pair", "core")
PIECES = ((0, 1), (2,))
ANYWHERE = pl.BlockSpec(memory_space=pl.ANY)
VMEM = pl.BlockSpec(memory_space=pltpu.VMEM)


def tile_of(slot):
    mirror = lax.axis_index("half") * (STAGES - 1)
    return lax.axis_index("stage") ^ mirror ^ slot


def exchange(block, slot):
    if slot == 0:
        return block
    return lax.ppermute(block, "stage", [(u, u ^ slot) for u in range(STAGES)])


def pick_kernel(levels, wanted_ref, history_ref, out_ref):
    rows = history_ref.shape[1]
    receivers, _, slots, width = out_ref.shape
    wanted = wanted_ref[...]
    column = lax.broadcasted_iota(jnp.int32, (receivers * slots, rows), 1)
    pick = jnp.where(wanted == column, 1.0, 0.0).astype(jnp.bfloat16)
    for place, i in enumerate(levels):
        got = jnp.dot(pick, history_ref[i], preferred_element_type=jnp.float32)
        out_ref[:, place] = got.astype(jnp.bfloat16).reshape(receivers, slots, width)


def pick_rows(levels, wanted, history, parts, slots):
    width = history.shape[2]
    step = 16
    return pl.pallas_call(
        lambda *refs: pick_kernel(levels, *refs),
        out_shape=jax.ShapeDtypeStruct((parts, len(levels), slots, width), jnp.bfloat16),
        grid=(parts // step,),
        in_specs=[
            pl.BlockSpec((step * slots, 1), lambda g: (g, 0)),
            pl.BlockSpec(history.shape, lambda g: (0, 0, 0)),
        ],
        out_specs=pl.BlockSpec((step, len(levels), slots, width), lambda g: (g, 0, 0, 0)),
        compiler_params=pltpu.CompilerParams(vmem_limit_bytes=24 * 1024 * 1024),
        cost_estimate=pl.CostEstimate(
            flops=2 * len(levels) * parts * slots * history.shape[1] * width,
            bytes_accessed=2 * (len(levels) * parts * slots * width + history.size),
            transcendentals=0,
        ),
    )(wanted, history)


def halo_kernel(levels, arrived_ref, spread_ref, features_ref, *out_refs):
    parts, _, slots, width = arrived_ref.shape
    tiles, rows, _ = spread_ref.shape
    spread = jnp.concatenate([spread_ref[tile_of(r)] for r in range(tiles)], axis=0)
    for place in range(levels):
        halo = arrived_ref[:, place].reshape(parts * slots, width)
        summed = jnp.dot(spread, halo, preferred_element_type=jnp.float32)
        for r in range(tiles):
            start = 0.1 * features_ref[tile_of(r)].astype(jnp.float32)
            part = 0.9 * summed[r * rows : (r + 1) * rows] + start
            out_refs[r][place] = part.astype(jnp.bfloat16)


def halo_sums(arrived, spread, features):
    parts, levels, slots, width = arrived.shape
    tiles, rows, halo_rows = spread.shape
    return pl.pallas_call(
        lambda *refs: halo_kernel(levels, *refs),
        out_shape=[jax.ShapeDtypeStruct((levels, rows, width), jnp.bfloat16)] * tiles,
        in_specs=[VMEM] * 3,
        out_specs=[VMEM] * tiles,
        compiler_params=pltpu.CompilerParams(vmem_limit_bytes=24 * 1024 * 1024),
        cost_estimate=pl.CostEstimate(
            flops=2 * levels * tiles * rows * halo_rows * width,
            bytes_accessed=2 * (arrived.size + spread.size + features.size * (1 + levels)),
            transcendentals=0,
        ),
    )(arrived, spread, features)


def chain_kernel(which, betas, x_ref, a_ref, w_ref, *refs):
    stages, cores, levels, depth, width = w_ref.shape
    pieces = len(PIECES)
    h_refs = refs[: pieces * stages]
    refs = refs[pieces * stages :]
    if which > 0:
        before_refs, refs = refs[:stages], refs[stages:]
        out_refs, refs = refs[:stages], refs[stages:]
    else:
        out_refs, last_ref, refs = refs[:stages], refs[stages], refs[stages + 1 :]
    w_buf, w_sem, h_sem = refs[:3]
    h_bufs = refs[3:]
    half = lax.axis_index("half")
    stage = lax.axis_index("stage")

    @pl.when(half == which)
    def _():
        def w_copy(s, c):
            return pltpu.make_async_copy(
                w_ref.at[s, c], w_buf.at[s, :, pl.ds(c * depth, depth)], w_sem.at[s, c]
            )

        def h_copy(p, r, s):
            return pltpu.make_async_copy(
                h_refs[p * stages + r], h_bufs[p].at[s], h_sem.at[p, s]
            )

        for r in range(stages):
            for p in range(pieces):
                h_copy(p, r, stage ^ r).start()
        for s in range(stages):
            for c in range(cores):
                w_copy(s, c).start()

        a = a_ref[...]
        x = x_ref[...]
        for s in range(stages):
            for p in range(pieces):
                h_copy(p, 0, s).wait()
            for c in range(cores):
                w_copy(s, c).wait()
            for p, chosen in enumerate(PIECES):
                for place, i in enumerate(chosen):
                    beta = betas[(which * stages + s) * levels + i]
                    summed = jnp.dot(a, x, preferred_element_type=jnp.float32)
                    support = 0.9 * summed + h_bufs[p][s, place].astype(jnp.float32)
                    branch = jnp.dot(
                        support.astype(jnp.bfloat16),
                        w_buf[s, i],
                        preferred_element_type=jnp.float32,
                    )
                    mixed = (1.0 - beta) * support + beta * branch
                    x = jnp.maximum(mixed, 0.0).astype(jnp.bfloat16)
            for r in range(stages):

                @pl.when(stage ^ s == r)
                def _():
                    out_refs[r][...] = x

        if which == 0:
            last_ref[...] = x

    @pl.when(half != which)
    def _():
        if which == 0:
            last_ref[...] = jnp.zeros_like(last_ref)
        for r in range(stages):
            out_refs[r][...] = before_refs[r][...] if which > 0 else jnp.zeros_like(out_refs[r])


def chain(which, x, a, weights, halos, before=()):
    stages, cores, levels, depth, width = weights.shape
    rows = x.shape[0]
    order = np.arange(HALVES * stages * levels, dtype=np.float32)
    betas = [float(b) for b in np.log1p(np.float32(1.0) / (order + np.float32(1.0)))]
    flat = [h for piece in halos for h in piece]
    outs = stages if before else stages + 1
    return pl.pallas_call(
        lambda *refs: chain_kernel(which, betas, *refs),
        out_shape=[jax.ShapeDtypeStruct((rows, width), jnp.bfloat16)] * outs,
        in_specs=[VMEM, VMEM, ANYWHERE] + [ANYWHERE] * len(flat) + [VMEM] * len(before),
        out_specs=[VMEM] * outs,
        scratch_shapes=[
            pltpu.VMEM((stages, levels, cores * depth, width), jnp.bfloat16),
            pltpu.SemaphoreType.DMA((stages, cores)),
            pltpu.SemaphoreType.DMA((len(halos), stages)),
        ]
        + [pltpu.VMEM((stages,) + piece[0].shape, jnp.bfloat16) for piece in halos],
        compiler_params=pltpu.CompilerParams(vmem_limit_bytes=60 * 1024 * 1024),
        cost_estimate=pl.CostEstimate(
            flops=2 * stages * levels * rows * width * (width + rows),
            bytes_accessed=2 * stages * levels * width * (width + rows),
            transcendentals=0,
        ),
    )(x, a, weights, *flat, *before)


def place_kernel(*refs):
    in_refs, out_ref, sem = refs[:-2], refs[-2], refs[-1]
    copies = [
        pltpu.make_async_copy(ref, out_ref.at[0, tile_of(r)], sem.at[r])
        for r, ref in enumerate(in_refs)
    ]
    for copy in copies:
        copy.start()
    for copy in copies:
        copy.wait()


def place(tiles):
    rows, width = tiles[0].shape
    return pl.pallas_call(
        place_kernel,
        out_shape=jax.ShapeDtypeStruct((1, len(tiles), rows, width), jnp.bfloat16),
        in_specs=[ANYWHERE] * len(tiles),
        out_specs=ANYWHERE,
        scratch_shapes=[pltpu.SemaphoreType.DMA((len(tiles),))],
    )(*tiles)


def local(features, history, weights, send_rows, send_count, adj_src, adj_blocks):
    rows_dev, width = features.shape
    levels = weights.shape[0]
    tile_rows = adj_blocks.shape[2]
    parts, slots = send_rows.shape[1:]
    halo_rows = parts * slots
    halo_tiles = halo_rows // tile_rows
    core = lax.axis_index("core")
    tiles = features.reshape(STAGES, tile_rows, width)

    depth = width // CORES
    own = lax.dynamic_slice_in_dim(weights, core * depth, depth, 1)
    group = lax.all_gather(own, ("stage", "core")).reshape(STAGES, CORES, levels, depth, width)

    live = jnp.arange(slots)[None, :] < send_count[0][:, None]
    wanted = jnp.where(live, send_rows[0], -1).reshape(halo_rows, 1)

    spread = sum(
        jnp.where(
            (adj_src[:, k, None] - 1 == jnp.arange(halo_tiles)[None, :])[:, None, :, None],
            adj_blocks[:, k, :, None, :],
            jnp.zeros((), jnp.bfloat16),
        )
        for k in range(1, adj_src.shape[1])
    ).reshape(STAGES, tile_rows, halo_rows)

    halos = []
    arrived = None
    for chosen in PIECES:
        outgoing = pick_rows(chosen, wanted, history, parts, slots)
        if arrived is not None:
            outgoing, arrived = lax.optimization_barrier((outgoing, arrived))
        following = lax.all_to_all(outgoing, DOM, split_axis=0, concat_axis=0, tiled=True)
        if arrived is not None:
            sums = halo_sums(arrived, spread, tiles)
            halos.append([exchange(block, r) for r, block in enumerate(sums)])
        arrived = following
    sums = halo_sums(arrived, spread, tiles)
    halos.append([exchange(block, r) for r, block in enumerate(sums)])

    own_tile = tile_of(0)
    x = lax.dynamic_index_in_dim(tiles, own_tile, 0, keepdims=False)
    a = lax.dynamic_index_in_dim(adj_blocks[:, 0], own_tile, 0, keepdims=False)
    *first, last = chain(0, x, a, group, halos)
    mirror = [(s, HALVES * STAGES - 1 - s) for s in range(STAGES)]
    done = chain(1, lax.ppermute(last, SEGMENT, mirror), a, group, halos, first)
    fresh = place([exchange(block, r) for r, block in enumerate(done)])
    return fresh.reshape(1, rows_dev, width)


def solution(mesh):
    segments, parts = mesh.devices.shape
    devices = mesh.devices.reshape(HALVES, segments // HALVES, parts // CORES, CORES)
    fine = Mesh(devices, SEGMENT + DOM)
    placed = (
        P(DOM, None),
        P(SEGMENT, DOM, None),
        P(SEGMENT, None, None),
        P(DOM, None, None),
        P(DOM, None),
        P(DOM, None),
        P(DOM, None, None, None),
    )
    return jax.shard_map(
        local, mesh=fine, in_specs=placed, out_specs=P(SEGMENT, DOM, None), check_vma=False
    )
```

```python
import jax
import jax.numpy as jnp
import numpy as np
from jax import lax
from jax.experimental import pallas as pl
from jax.experimental.pallas import tpu as pltpu
from jax.sharding import Mesh, PartitionSpec as P

HALVES = 2
STAGES = 4
CORES = 2
SEGMENT = ("half", "stage")
DOM = ("pair", "core")
PIECES = ((0, 1), (2,))
ANYWHERE = pl.BlockSpec(memory_space=pl.ANY)
VMEM = pl.BlockSpec(memory_space=pltpu.VMEM)
GRANT = pltpu.CompilerParams(vmem_limit_bytes=60 * 1024 * 1024)
SMALL = pltpu.CompilerParams(vmem_limit_bytes=24 * 1024 * 1024)


def tile_of(slot):
    mirror = lax.axis_index("half") * (STAGES - 1)
    return lax.axis_index("stage") ^ mirror ^ slot


def exchange(block, slot):
    if slot == 0:
        return block
    return lax.ppermute(block, "stage", [(u, u ^ slot) for u in range(STAGES)])


def spread_kernel(source_ref, blocks_ref, features_ref, out_ref, own_a_ref, own_x_ref):
    tiles, picked, rows, _ = blocks_ref.shape
    own_a_ref[...] = blocks_ref[tile_of(0), 0]
    own_x_ref[...] = features_ref[tile_of(0)]
    out_ref[...] = jnp.zeros_like(out_ref)
    for t in range(tiles):
        for k in range(1, picked):
            first = pl.multiple_of((source_ref[t, k] - 1) * rows, rows)
            out_ref[t, :, pl.ds(first, rows)] = blocks_ref[t, k]


def spread_blocks(adj_src, adj_blocks, features, halo_rows):
    tiles, _, rows, _ = adj_blocks.shape
    width = features.shape[2]
    return pl.pallas_call(
        spread_kernel,
        out_shape=[
            jax.ShapeDtypeStruct((tiles, rows, halo_rows), jnp.bfloat16),
            jax.ShapeDtypeStruct((rows, rows), jnp.bfloat16),
            jax.ShapeDtypeStruct((rows, width), jnp.bfloat16),
        ],
        in_specs=[pl.BlockSpec(memory_space=pltpu.SMEM), VMEM, VMEM],
        out_specs=[VMEM] * 3,
        compiler_params=GRANT,
    )(adj_src, adj_blocks, features)


def pick_kernel(rows_ref, count_ref, history_ref, out_ref):
    receivers, levels, slots, width = out_ref.shape
    rows = history_ref.shape[1]
    slot = lax.broadcasted_iota(jnp.int32, (slots, receivers), 0)
    wanted = jnp.where(slot < count_ref[0], rows_ref[0], -1)
    column = lax.broadcasted_iota(jnp.int32, (slots, rows), 1)
    picks = [
        jnp.where(wanted[:, p : p + 1] == column, 1.0, 0.0).astype(jnp.bfloat16)
        for p in range(receivers)
    ]
    pick = jnp.concatenate(picks, axis=0)
    for place in range(levels):
        got = jnp.dot(pick, history_ref[place], preferred_element_type=jnp.float32)
        out_ref[:, place] = got.astype(jnp.bfloat16).reshape(receivers, slots, width)


def pick_rows(levels, send_rows, send_count, history):
    parts, slots = send_rows.shape[1:]
    _, rows, width = history.shape
    step = 16
    steps = parts // step
    by_slot = send_rows.reshape(steps, step, slots).swapaxes(1, 2)
    return pl.pallas_call(
        pick_kernel,
        out_shape=jax.ShapeDtypeStruct((parts, len(levels), slots, width), jnp.bfloat16),
        grid=(steps,),
        in_specs=[
            pl.BlockSpec((1, slots, step), lambda g: (g, 0, 0)),
            pl.BlockSpec((1, 1, step), lambda g: (g, 0, 0)),
            pl.BlockSpec(
                (len(levels), rows, width), lambda g: (levels[0] // len(levels), 0, 0)
            ),
        ],
        out_specs=pl.BlockSpec((step, len(levels), slots, width), lambda g: (g, 0, 0, 0)),
        compiler_params=GRANT,
        cost_estimate=pl.CostEstimate(
            flops=2 * len(levels) * parts * slots * rows * width,
            bytes_accessed=2 * len(levels) * (parts * slots + rows) * width,
            transcendentals=0,
        ),
    )(by_slot, send_count.reshape(steps, 1, step), history)


def halo_kernel(levels, arrived_ref, spread_ref, features_ref, *out_refs):
    parts, _, slots, width = arrived_ref.shape
    tiles, rows, _ = spread_ref.shape
    spread = jnp.concatenate([spread_ref[tile_of(r)] for r in range(tiles)], axis=0)
    for place in range(levels):
        halo = arrived_ref[:, place].reshape(parts * slots, width)
        summed = jnp.dot(spread, halo, preferred_element_type=jnp.float32)
        for r in range(tiles):
            start = 0.1 * features_ref[tile_of(r)].astype(jnp.float32)
            part = 0.9 * summed[r * rows : (r + 1) * rows] + start
            out_refs[r][place] = part.astype(jnp.bfloat16)


def halo_sums(arrived, spread, features, grant):
    parts, levels, slots, width = arrived.shape
    tiles, rows, halo_rows = spread.shape
    return pl.pallas_call(
        lambda *refs: halo_kernel(levels, *refs),
        out_shape=[jax.ShapeDtypeStruct((levels, rows, width), jnp.bfloat16)] * tiles,
        in_specs=[VMEM] * 3,
        out_specs=[VMEM] * tiles,
        compiler_params=grant,
        cost_estimate=pl.CostEstimate(
            flops=2 * levels * tiles * rows * halo_rows * width,
            bytes_accessed=2 * (arrived.size + spread.size + features.size * (1 + levels)),
            transcendentals=0,
        ),
    )(arrived, spread, features)


def chain_kernel(which, betas, x_ref, a_ref, w_ref, *refs):
    stages, cores, levels, depth, _ = w_ref.shape
    pieces = len(PIECES)
    h_refs = [refs[p * stages : (p + 1) * stages] for p in range(pieces)]
    refs = refs[pieces * stages :]
    if which > 0:
        before_refs, refs = refs[:stages], refs[stages:]
    out_refs = refs[:stages]
    h_bufs = refs[-pieces:]
    half = lax.axis_index("half")
    stage = lax.axis_index("stage")

    @pl.when(half == which)
    def _():
        for p in range(pieces):
            for r in range(stages):
                h_bufs[p][stage ^ r] = h_refs[p][r][...]
        a = a_ref[...]
        x = x_ref[...]
        for s in range(stages):
            for p, chosen in enumerate(PIECES):
                for place, i in enumerate(chosen):
                    beta = betas[(which * stages + s) * levels + i]
                    summed = jnp.dot(a, x, preferred_element_type=jnp.float32)
                    support = 0.9 * summed + h_bufs[p][s, place].astype(jnp.float32)
                    rounded = support.astype(jnp.bfloat16)
                    branch = sum(
                        jnp.dot(
                            rounded[:, c * depth : (c + 1) * depth],
                            w_ref[s, c, i],
                            preferred_element_type=jnp.float32,
                        )
                        for c in range(cores)
                    )
                    mixed = (1.0 - beta) * support + beta * branch
                    x = jnp.maximum(mixed, 0.0).astype(jnp.bfloat16)
            for r in range(stages):

                @pl.when(stage ^ s == r)
                def _():
                    out_refs[r][...] = x

        if which == 0:
            refs[stages][...] = x

    if which > 0:

        @pl.when(half != which)
        def _():
            for r in range(stages):
                out_refs[r][...] = before_refs[r][...]


def chain(which, x, a, weights, halos, before=()):
    stages, _, levels, _, width = weights.shape
    rows = x.shape[0]
    order = np.arange(HALVES * stages * levels, dtype=np.float32)
    betas = [float(b) for b in np.log1p(np.float32(1.0) / (order + np.float32(1.0)))]
    flat = [h for piece in halos for h in piece]
    outs = stages if before else stages + 1
    return pl.pallas_call(
        lambda *refs: chain_kernel(which, betas, *refs),
        out_shape=[jax.ShapeDtypeStruct((rows, width), jnp.bfloat16)] * outs,
        in_specs=[VMEM] * (3 + len(flat) + len(before)),
        out_specs=[VMEM] * outs,
        scratch_shapes=[
            pltpu.VMEM((stages,) + piece[0].shape, jnp.bfloat16) for piece in halos
        ],
        compiler_params=SMALL,
        cost_estimate=pl.CostEstimate(
            flops=2 * stages * levels * rows * width * (width + rows),
            bytes_accessed=2 * stages * levels * width * (width + rows),
            transcendentals=0,
        ),
    )(x, a, weights, *flat, *before)


def place_kernel(*refs):
    in_refs, out_ref = refs[:-1], refs[-1]
    for r, ref in enumerate(in_refs):
        out_ref[0, tile_of(r)] = ref[...]


def place(tiles):
    rows, width = tiles[0].shape
    return pl.pallas_call(
        place_kernel,
        out_shape=jax.ShapeDtypeStruct((1, len(tiles), rows, width), jnp.bfloat16),
        in_specs=[VMEM] * len(tiles),
        out_specs=VMEM,
        compiler_params=SMALL,
    )(*tiles)


def local(features, history, weights, send_rows, send_count, adj_src, adj_blocks):
    rows_dev, width = features.shape
    levels = weights.shape[0]
    tile_rows = adj_blocks.shape[2]
    parts, slots = send_rows.shape[1:]
    halo_rows = parts * slots
    core = lax.axis_index("core")
    tiles = features.reshape(STAGES, tile_rows, width)

    outgoing = pick_rows(PIECES[0], send_rows, send_count, history)
    outgoing, history, adj_blocks = lax.optimization_barrier((outgoing, history, adj_blocks))
    spread, own_a, own_x = spread_blocks(adj_src, adj_blocks, tiles, halo_rows)
    spread, weights = lax.optimization_barrier((spread, weights))

    depth = width // CORES
    own = lax.dynamic_slice_in_dim(weights, core * depth, depth, 1)
    group = lax.all_gather(own, ("stage", "core")).reshape(STAGES, CORES, levels, depth, width)

    halos = []
    for following in PIECES[1:] + (None,):
        arrived = lax.all_to_all(outgoing, DOM, split_axis=0, concat_axis=0, tiled=True)
        if following is not None:
            outgoing = pick_rows(following, send_rows, send_count, history)
            arrived, outgoing, spread = lax.optimization_barrier((arrived, outgoing, spread))
        sums = halo_sums(arrived, spread, tiles, SMALL)
        if following is None:
            sums, group = lax.optimization_barrier((sums, group))
        halos.append([exchange(block, r) for r, block in enumerate(sums)])

    *first, last = chain(0, own_x, own_a, group, halos)
    mirror = [(s, HALVES * STAGES - 1 - s) for s in range(STAGES)]
    done = chain(1, lax.ppermute(last, SEGMENT, mirror), own_a, group, halos, first)
    fresh = place([exchange(block, r) for r, block in enumerate(done)])
    return fresh.reshape(1, rows_dev, width)


def solution(mesh):
    segments, parts = mesh.devices.shape
    devices = mesh.devices.reshape(HALVES, segments // HALVES, parts // CORES, CORES)
    fine = Mesh(devices, SEGMENT + DOM)
    placed = (
        P(DOM, None),
        P(SEGMENT, DOM, None),
        P(SEGMENT, None, None),
        P(DOM, None, None),
        P(DOM, None),
        P(DOM, None),
        P(DOM, None, None, None),
    )
    return jax.shard_map(
        local, mesh=fine, in_specs=placed, out_specs=P(SEGMENT, DOM, None), check_vma=False
    )
```

```python
import jax
import jax.numpy as jnp
import numpy as np
from jax import lax
from jax.experimental import pallas as pl
from jax.experimental.pallas import tpu as pltpu
from jax.sharding import Mesh, PartitionSpec as P

HALVES = 2
STAGES = 4
CORES = 2
SEGMENT = ("half", "stage")
DOM = ("pair", "core")
PIECES = ((0, 1), (2,))
ANYWHERE = pl.BlockSpec(memory_space=pl.ANY)
VMEM = pl.BlockSpec(memory_space=pltpu.VMEM)
GRANT = pltpu.CompilerParams(vmem_limit_bytes=60 * 1024 * 1024)
SMALL = pltpu.CompilerParams(vmem_limit_bytes=24 * 1024 * 1024)


def tile_of(slot):
    mirror = lax.axis_index("half") * (STAGES - 1)
    return lax.axis_index("stage") ^ mirror ^ slot


def exchange(block, slot):
    if slot == 0:
        return block
    return lax.ppermute(block, "stage", [(u, u ^ slot) for u in range(STAGES)])


def spread_kernel(source_ref, blocks_ref, out_ref):
    tiles, picked, rows, _ = blocks_ref.shape
    out_ref[...] = jnp.zeros_like(out_ref)
    for t in range(tiles):
        for k in range(1, picked):
            first = pl.multiple_of((source_ref[t, k] - 1) * rows, rows)
            out_ref[t, :, pl.ds(first, rows)] = blocks_ref[t, k]


def spread_blocks(adj_src, adj_blocks, halo_rows):
    tiles, _, rows, _ = adj_blocks.shape
    return pl.pallas_call(
        spread_kernel,
        out_shape=jax.ShapeDtypeStruct((tiles, rows, halo_rows), jnp.bfloat16),
        in_specs=[pl.BlockSpec(memory_space=pltpu.SMEM), VMEM],
        out_specs=VMEM,
        compiler_params=GRANT,
    )(adj_src, adj_blocks)


def pick_kernel(rows_ref, count_ref, history_ref, out_ref, pick_ref):
    receivers, _, slots, width = out_ref.shape
    rows = history_ref.shape[1]

    @pl.when(pl.program_id(0) == 0)
    def _():
        slot = lax.broadcasted_iota(jnp.int32, (slots, receivers), 0)
        wanted = jnp.where(slot < count_ref[...], rows_ref[0], -1)
        column = lax.broadcasted_iota(jnp.int32, (slots, rows), 1)
        for p in range(receivers):
            mask = jnp.where(wanted[:, p : p + 1] == column, 1.0, 0.0)
            pick_ref[p * slots : (p + 1) * slots] = mask.astype(jnp.bfloat16)

    got = jnp.dot(pick_ref[...], history_ref[0], preferred_element_type=jnp.float32)
    out_ref[:, 0] = got.astype(jnp.bfloat16).reshape(receivers, slots, width)


def pick_rows(levels, send_rows, send_count, history):
    parts, slots = send_rows.shape[1:]
    _, rows, width = history.shape
    return pl.pallas_call(
        pick_kernel,
        out_shape=jax.ShapeDtypeStruct((parts, len(levels), slots, width), jnp.bfloat16),
        grid=(len(levels),),
        in_specs=[
            pl.BlockSpec((1, slots, parts), lambda g: (0, 0, 0)),
            pl.BlockSpec((1, parts), lambda g: (0, 0)),
            pl.BlockSpec((1, rows, width), lambda g: (levels[0] + g, 0, 0)),
        ],
        out_specs=pl.BlockSpec((parts, 1, slots, width), lambda g: (0, g, 0, 0)),
        scratch_shapes=[pltpu.VMEM((parts * slots, rows), jnp.bfloat16)],
        compiler_params=GRANT,
        cost_estimate=pl.CostEstimate(
            flops=2 * len(levels) * parts * slots * rows * width,
            bytes_accessed=2 * len(levels) * (parts * slots + rows) * width,
            transcendentals=0,
        ),
    )(send_rows.swapaxes(1, 2), send_count, history)


def stage_kernel(*refs):
    sources, outs, sem = refs[: 2 * STAGES + 2], refs[2 * STAGES + 2 : -1], refs[-1]
    own_ref, near_refs, far_refs = sources[0], sources[1:STAGES], sources[STAGES : 2 * STAGES - 1]
    features_ref, blocks_ref, spread_ref = sources[2 * STAGES - 1 :]
    group_ref, own_x_ref, own_a_ref, spread_out = outs
    depth = group_ref.shape[3]
    stage = lax.axis_index("stage")
    core = lax.axis_index("core")
    pairs = [
        (spread_ref, spread_out),
        (features_ref.at[tile_of(0)], own_x_ref),
        (blocks_ref.at[tile_of(0), 0], own_a_ref),
    ]
    for c in range(CORES):
        pairs.append((own_ref.at[:, pl.ds(c * depth, depth)], group_ref.at[stage, c]))
    for r in range(1, STAGES):
        pairs.append((near_refs[r - 1], group_ref.at[stage ^ r, core]))
        pairs.append((far_refs[r - 1], group_ref.at[stage ^ r, 1 - core]))
    copies = [pltpu.make_async_copy(*pair, sem.at[n]) for n, pair in enumerate(pairs)]
    for copy in copies:
        copy.start()
    for copy in copies:
        copy.wait()


def stage_operands(weights, near, far, features, adj_blocks, spread):
    levels, width, _ = weights.shape
    tiles, rows, _ = spread.shape
    sources = [weights, *near, *far, features, adj_blocks, spread]
    shapes = [
        (STAGES, CORES, levels, width // CORES, width),
        (rows, width),
        (rows, rows),
        spread.shape,
    ]
    return pl.pallas_call(
        stage_kernel,
        out_shape=[jax.ShapeDtypeStruct(shape, jnp.bfloat16) for shape in shapes],
        in_specs=[ANYWHERE] * len(sources),
        out_specs=[VMEM] * len(shapes),
        scratch_shapes=[pltpu.SemaphoreType.DMA((2 * STAGES + CORES + 1,))],
        compiler_params=SMALL,
    )(*sources)


def halo_kernel(levels, arrived_ref, spread_ref, features_ref, *out_refs):
    parts, _, slots, width = arrived_ref.shape
    tiles, rows, _ = spread_ref.shape
    spread = jnp.concatenate([spread_ref[tile_of(r)] for r in range(tiles)], axis=0)
    for place in range(levels):
        halo = arrived_ref[:, place].reshape(parts * slots, width)
        summed = jnp.dot(spread, halo, preferred_element_type=jnp.float32)
        for r in range(tiles):
            start = 0.1 * features_ref[tile_of(r)].astype(jnp.float32)
            part = 0.9 * summed[r * rows : (r + 1) * rows] + start
            out_refs[r][place] = part.astype(jnp.bfloat16)


def halo_sums(arrived, spread, features, grant):
    parts, levels, slots, width = arrived.shape
    tiles, rows, halo_rows = spread.shape
    return pl.pallas_call(
        lambda *refs: halo_kernel(levels, *refs),
        out_shape=[jax.ShapeDtypeStruct((levels, rows, width), jnp.bfloat16)] * tiles,
        in_specs=[VMEM] * 3,
        out_specs=[VMEM] * tiles,
        compiler_params=grant,
        cost_estimate=pl.CostEstimate(
            flops=2 * levels * tiles * rows * halo_rows * width,
            bytes_accessed=2 * (arrived.size + spread.size + features.size * (1 + levels)),
            transcendentals=0,
        ),
    )(arrived, spread, features)


def chain_kernel(which, betas, x_ref, a_ref, w_ref, *refs):
    stages, cores, levels, depth, _ = w_ref.shape
    pieces = len(PIECES)
    h_refs = [refs[p * stages : (p + 1) * stages] for p in range(pieces)]
    refs = refs[pieces * stages :]
    if which > 0:
        before_refs, refs = refs[:stages], refs[stages:]
    out_refs = refs[:stages]
    h_bufs = refs[-pieces:]
    half = lax.axis_index("half")
    stage = lax.axis_index("stage")

    @pl.when(half == which)
    def _():
        for p in range(pieces):
            for r in range(stages):
                h_bufs[p][stage ^ r] = h_refs[p][r][...]
        a = a_ref[...]
        x = x_ref[...]
        for s in range(stages):
            for p, chosen in enumerate(PIECES):
                for place, i in enumerate(chosen):
                    beta = betas[(which * stages + s) * levels + i]
                    summed = jnp.dot(a, x, preferred_element_type=jnp.float32)
                    support = 0.9 * summed + h_bufs[p][s, place].astype(jnp.float32)
                    rounded = support.astype(jnp.bfloat16)
                    branch = sum(
                        jnp.dot(
                            rounded[:, c * depth : (c + 1) * depth],
                            w_ref[s, c, i],
                            preferred_element_type=jnp.float32,
                        )
                        for c in range(cores)
                    )
                    mixed = (1.0 - beta) * support + beta * branch
                    x = jnp.maximum(mixed, 0.0).astype(jnp.bfloat16)
            for r in range(stages):

                @pl.when(stage ^ s == r)
                def _():
                    out_refs[r][...] = x

        if which == 0:
            refs[stages][...] = x

    if which > 0:

        @pl.when(half != which)
        def _():
            for r in range(stages):
                out_refs[r][...] = before_refs[r][...]


def chain(which, x, a, weights, halos, before=()):
    stages, _, levels, _, width = weights.shape
    rows = x.shape[0]
    order = np.arange(HALVES * stages * levels, dtype=np.float32)
    betas = [float(b) for b in np.log1p(np.float32(1.0) / (order + np.float32(1.0)))]
    flat = [h for piece in halos for h in piece]
    outs = stages if before else stages + 1
    return pl.pallas_call(
        lambda *refs: chain_kernel(which, betas, *refs),
        out_shape=[jax.ShapeDtypeStruct((rows, width), jnp.bfloat16)] * outs,
        in_specs=[VMEM] * (3 + len(flat) + len(before)),
        out_specs=[VMEM] * outs,
        scratch_shapes=[
            pltpu.VMEM((stages,) + piece[0].shape, jnp.bfloat16) for piece in halos
        ],
        compiler_params=SMALL,
        cost_estimate=pl.CostEstimate(
            flops=2 * stages * levels * rows * width * (width + rows),
            bytes_accessed=2 * stages * levels * width * (width + rows),
            transcendentals=0,
        ),
    )(x, a, weights, *flat, *before)


def place_kernel(*refs):
    in_refs, out_ref = refs[:-1], refs[-1]
    for r, ref in enumerate(in_refs):
        out_ref[0, tile_of(r)] = ref[...]


def place(tiles):
    rows, width = tiles[0].shape
    return pl.pallas_call(
        place_kernel,
        out_shape=jax.ShapeDtypeStruct((1, len(tiles), rows, width), jnp.bfloat16),
        in_specs=[VMEM] * len(tiles),
        out_specs=VMEM,
        compiler_params=SMALL,
    )(*tiles)


def local(features, history, weights, send_rows, send_count, adj_src, adj_blocks):
    rows_dev, width = features.shape
    tile_rows = adj_blocks.shape[2]
    parts, slots = send_rows.shape[1:]
    halo_rows = parts * slots
    tiles = features.reshape(STAGES, tile_rows, width)

    outgoing = pick_rows(PIECES[0], send_rows, send_count, history)
    outgoing, history, adj_blocks, weights = lax.optimization_barrier(
        (outgoing, history, adj_blocks, weights)
    )
    arrived = lax.all_to_all(outgoing, DOM, split_axis=0, concat_axis=0, tiled=True)

    depth = weights.shape[1] // CORES
    core = lax.axis_index("core")
    own = lax.dynamic_slice_in_dim(weights, core * depth, depth, 1)
    near = [exchange(own, r) for r in range(1, STAGES)]
    spread = spread_blocks(adj_src, adj_blocks, halo_rows)
    outgoing = pick_rows(PIECES[1], send_rows, send_count, history)
    arrived, outgoing, spread = lax.optimization_barrier((arrived, outgoing, spread))

    following = lax.all_to_all(outgoing, DOM, split_axis=0, concat_axis=0, tiled=True)
    sums = halo_sums(arrived, spread, tiles, SMALL)
    near, token = lax.optimization_barrier((near, sums[0]))
    sums = [token, *sums[1:]]
    far = [lax.ppermute(block, "core", [(0, 1), (1, 0)]) for block in near]
    halos = [[exchange(block, r) for r, block in enumerate(sums)]]
    group, own_x, own_a, spread = stage_operands(weights, near, far, tiles, adj_blocks, spread)
    sums = halo_sums(following, spread, tiles, SMALL)
    halos.append([exchange(block, r) for r, block in enumerate(sums)])

    *first, last = chain(0, own_x, own_a, group, halos)
    mirror = [(s, HALVES * STAGES - 1 - s) for s in range(STAGES)]
    done = chain(1, lax.ppermute(last, SEGMENT, mirror), own_a, group, halos, first)
    fresh = place([exchange(block, r) for r, block in enumerate(done)])
    return fresh.reshape(1, rows_dev, width)


def solution(mesh):
    segments, parts = mesh.devices.shape
    devices = mesh.devices.reshape(HALVES, segments // HALVES, parts // CORES, CORES)
    fine = Mesh(devices, SEGMENT + DOM)
    placed = (
        P(DOM, None),
        P(SEGMENT, DOM, None),
        P(SEGMENT, None, None),
        P(DOM, None, None),
        P(DOM, None),
        P(DOM, None),
        P(DOM, None, None, None),
    )
    return jax.shard_map(
        local, mesh=fine, in_specs=placed, out_specs=P(SEGMENT, DOM, None), check_vma=False
    )
```

```python
import jax
import jax.numpy as jnp
import numpy as np
from jax import lax
from jax.experimental import pallas as pl
from jax.experimental.pallas import tpu as pltpu
from jax.sharding import Mesh, PartitionSpec as P

HALVES = 2
STAGES = 4
CORES = 2
SEGMENT = ("half", "stage")
DOM = ("pair", "core")
ANYWHERE = pl.BlockSpec(memory_space=pl.ANY)
VMEM = pl.BlockSpec(memory_space=pltpu.VMEM)
GRANT = pltpu.CompilerParams(vmem_limit_bytes=60 * 1024 * 1024)
SMALL = pltpu.CompilerParams(vmem_limit_bytes=24 * 1024 * 1024)


def tile_of(slot):
    mirror = lax.axis_index("half") * (STAGES - 1)
    return lax.axis_index("stage") ^ mirror ^ slot


def exchange(block, slot):
    return lax.ppermute(block, "stage", [(u, u ^ slot) for u in range(STAGES)])


def exchange_all(blocks):
    return [blocks[0]] + [exchange(blocks[slot], slot) for slot in range(1, STAGES)]


def swap_cores(block):
    return lax.ppermute(block, "core", [(0, 1), (1, 0)])


def spread_kernel(source_ref, blocks_ref, out_ref):
    tiles, picked, rows, _ = blocks_ref.shape
    out_ref[...] = jnp.zeros_like(out_ref)
    for t in range(tiles):
        for k in range(1, picked):
            first = pl.multiple_of((source_ref[t, k] - 1) * rows, rows)
            out_ref[t, :, pl.ds(first, rows)] = blocks_ref[t, k]


def spread_blocks(adj_src, adj_blocks, halo_rows):
    tiles, _, rows, _ = adj_blocks.shape
    return pl.pallas_call(
        spread_kernel,
        out_shape=jax.ShapeDtypeStruct((tiles, rows, halo_rows), jnp.bfloat16),
        in_specs=[pl.BlockSpec(memory_space=pltpu.SMEM), VMEM],
        out_specs=VMEM,
        compiler_params=GRANT,
    )(adj_src, adj_blocks)


def pick_kernel(rows_ref, count_ref, history_ref, out_ref, pick_ref):
    receivers, _, slots, width = out_ref.shape
    rows = history_ref.shape[1]

    @pl.when(pl.program_id(0) == 0)
    def _():
        slot = lax.broadcasted_iota(jnp.int32, (slots, receivers), 0)
        wanted = jnp.where(slot < count_ref[...], rows_ref[0], -1)
        column = lax.broadcasted_iota(jnp.int32, (slots, rows), 1)
        for p in range(receivers):
            mask = jnp.where(wanted[:, p : p + 1] == column, 1.0, 0.0)
            pick_ref[p * slots : (p + 1) * slots] = mask.astype(jnp.bfloat16)

    got = jnp.dot(pick_ref[...], history_ref[0], preferred_element_type=jnp.float32)
    out_ref[:, 0] = got.astype(jnp.bfloat16).reshape(receivers, slots, width)


def pick_rows(send_rows, send_count, history):
    parts, slots = send_rows.shape[1:]
    levels, rows, width = history.shape
    return pl.pallas_call(
        pick_kernel,
        out_shape=jax.ShapeDtypeStruct((parts, levels, slots, width), jnp.bfloat16),
        grid=(levels,),
        in_specs=[
            pl.BlockSpec((1, slots, parts), lambda g: (0, 0, 0)),
            pl.BlockSpec((1, parts), lambda g: (0, 0)),
            pl.BlockSpec((1, rows, width), lambda g: (g, 0, 0)),
        ],
        out_specs=pl.BlockSpec((parts, 1, slots, width), lambda g: (0, g, 0, 0)),
        scratch_shapes=[pltpu.VMEM((parts * slots, rows), jnp.bfloat16)],
        compiler_params=GRANT,
        cost_estimate=pl.CostEstimate(
            flops=2 * levels * parts * slots * rows * width,
            bytes_accessed=2 * levels * (parts * slots + rows) * width,
            transcendentals=0,
        ),
    )(send_rows.swapaxes(1, 2), send_count, history)


def stage_kernel(*refs):
    shards = STAGES
    own_ref, near_refs, far_refs = refs[0], refs[1 : 1 + shards], refs[1 + shards : 1 + 2 * shards]
    features_ref, blocks_ref, group_ref, own_x_ref, own_a_ref, sem = refs[1 + 2 * shards :]
    depth = group_ref.shape[3]
    stage = lax.axis_index("stage")
    core = lax.axis_index("core")
    pairs = [
        (features_ref.at[tile_of(0)], own_x_ref),
        (blocks_ref.at[tile_of(0), 0], own_a_ref),
    ]
    for c in range(CORES):
        pairs.append((own_ref.at[:, pl.ds(c * depth, depth)], group_ref.at[stage, c]))
    for r in range(1, STAGES):
        pairs.append((near_refs[r - 1], group_ref.at[stage ^ r, core]))
        pairs.append((far_refs[r - 1], group_ref.at[stage ^ r, 1 - core]))
    copies = [pltpu.make_async_copy(*pair, sem.at[n]) for n, pair in enumerate(pairs)]
    late = len(copies) - 2
    inner = (stage == 1) | (stage == 2)
    for copy in copies[:late]:
        copy.start()

    @pl.when(inner)
    def _():
        for copy in copies[late:]:
            copy.start()

    @pl.when(jnp.logical_not(inner))
    def _():
        pltpu.make_async_copy(near_refs[-1], pairs[late][1], sem.at[late]).start()
        pltpu.make_async_copy(far_refs[-1], pairs[late + 1][1], sem.at[late + 1]).start()

    for copy in copies:
        copy.wait()


def stage_operands(weights, near, far, features, adj_blocks):
    levels, width, _ = weights.shape
    rows = adj_blocks.shape[2]
    sources = [weights, *near, *far, features, adj_blocks]
    shapes = [(STAGES, CORES, levels, width // CORES, width), (rows, width), (rows, rows)]
    return pl.pallas_call(
        stage_kernel,
        out_shape=[jax.ShapeDtypeStruct(shape, jnp.bfloat16) for shape in shapes],
        in_specs=[ANYWHERE] * len(sources),
        out_specs=[VMEM] * len(shapes),
        scratch_shapes=[pltpu.SemaphoreType.DMA((2 * STAGES + CORES,))],
        compiler_params=SMALL,
        cost_estimate=pl.CostEstimate(
            flops=0, bytes_accessed=4 * STAGES * weights.size, transcendentals=0
        ),
    )(*sources)


def halo_kernel(arrived_ref, spread_ref, features_ref, *out_refs):
    parts, _, slots, width = arrived_ref.shape
    tiles, rows, _ = spread_ref.shape
    spread = jnp.concatenate([spread_ref[tile_of(r)] for r in range(tiles)], axis=0)
    halo = arrived_ref[:, 0].reshape(parts * slots, width)
    summed = jnp.dot(spread, halo, preferred_element_type=jnp.float32)
    for r in range(tiles):
        start = 0.1 * features_ref[tile_of(r)].astype(jnp.float32)
        part = 0.9 * summed[r * rows : (r + 1) * rows] + start
        out_refs[r][0] = part.astype(jnp.bfloat16)


def halo_sums(arrived, spread, features):
    parts, levels, slots, width = arrived.shape
    tiles, rows, halo_rows = spread.shape
    return pl.pallas_call(
        halo_kernel,
        out_shape=[jax.ShapeDtypeStruct((levels, rows, width), jnp.bfloat16)] * tiles,
        grid=(levels,),
        in_specs=[
            pl.BlockSpec((parts, 1, slots, width), lambda g: (0, g, 0, 0)),
            pl.BlockSpec(spread.shape, lambda g: (0, 0, 0)),
            pl.BlockSpec(features.shape, lambda g: (0, 0, 0)),
        ],
        out_specs=[pl.BlockSpec((1, rows, width), lambda g: (g, 0, 0))] * tiles,
        compiler_params=SMALL,
        cost_estimate=pl.CostEstimate(
            flops=2 * levels * tiles * rows * halo_rows * width,
            bytes_accessed=2 * (arrived.size + spread.size + features.size * (1 + levels)),
            transcendentals=0,
        ),
    )(arrived, spread, features)


def chain_kernel(which, betas, x_ref, a_ref, w_ref, *refs):
    stages, cores, levels, depth, _ = w_ref.shape
    h_refs, refs = refs[:stages], refs[stages:]
    if which > 0:
        before_refs, refs = refs[:stages], refs[stages:]
    out_refs, h_buf = refs[:stages], refs[-1]
    half = lax.axis_index("half")
    stage = lax.axis_index("stage")

    @pl.when(half == which)
    def _():
        for r in range(stages):
            h_buf[stage ^ r] = h_refs[r][...]
        a = a_ref[...]
        x = x_ref[...]
        for s in range(stages):
            for i in range(levels):
                beta = betas[(which * stages + s) * levels + i]
                summed = jnp.dot(a, x, preferred_element_type=jnp.float32)
                support = 0.9 * summed + h_buf[s, i].astype(jnp.float32)
                rounded = support.astype(jnp.bfloat16)
                branch = sum(
                    jnp.dot(
                        rounded[:, c * depth : (c + 1) * depth],
                        w_ref[s, c, i],
                        preferred_element_type=jnp.float32,
                    )
                    for c in range(cores)
                )
                mixed = (1.0 - beta) * support + beta * branch
                x = jnp.maximum(mixed, 0.0).astype(jnp.bfloat16)
            for r in range(stages):

                @pl.when(stage ^ s == r)
                def _():
                    out_refs[r][...] = x

        if which == 0:
            refs[stages][...] = x

    if which > 0:

        @pl.when(half != which)
        def _():
            for r in range(stages):
                out_refs[r][...] = before_refs[r][...]


def chain(which, x, a, weights, halos, before=()):
    stages, _, levels, _, width = weights.shape
    rows = x.shape[0]
    order = np.arange(HALVES * stages * levels, dtype=np.float32)
    betas = [float(b) for b in np.log1p(np.float32(1.0) / (order + np.float32(1.0)))]
    outs = stages if before else stages + 1
    return pl.pallas_call(
        lambda *refs: chain_kernel(which, betas, *refs),
        out_shape=[jax.ShapeDtypeStruct((rows, width), jnp.bfloat16)] * outs,
        in_specs=[VMEM] * (3 + len(halos) + len(before)),
        out_specs=[VMEM] * outs,
        scratch_shapes=[pltpu.VMEM((stages, levels, rows, width), jnp.bfloat16)],
        compiler_params=SMALL,
        cost_estimate=pl.CostEstimate(
            flops=2 * stages * levels * rows * width * (width + rows),
            bytes_accessed=2 * stages * levels * width * (width + rows),
            transcendentals=0,
        ),
    )(x, a, weights, *halos, *before)


def place_kernel(*refs):
    in_refs, out_ref = refs[:-1], refs[-1]
    for r, ref in enumerate(in_refs):
        out_ref[0, tile_of(r)] = ref[...]


def place(tiles):
    rows, width = tiles[0].shape
    return pl.pallas_call(
        place_kernel,
        out_shape=jax.ShapeDtypeStruct((1, len(tiles), rows, width), jnp.bfloat16),
        in_specs=[VMEM] * len(tiles),
        out_specs=VMEM,
        compiler_params=SMALL,
    )(*tiles)


def local(features, history, weights, send_rows, send_count, adj_src, adj_blocks):
    rows_dev, width = features.shape
    tile_rows = adj_blocks.shape[2]
    parts, slots = send_rows.shape[1:]
    halo_rows = parts * slots
    tiles = features.reshape(STAGES, tile_rows, width)

    outgoing = pick_rows(send_rows, send_count, history)
    outgoing, adj_blocks, weights = lax.optimization_barrier((outgoing, adj_blocks, weights))
    arrived = lax.all_to_all(outgoing, DOM, split_axis=0, concat_axis=0, tiled=True)

    depth = weights.shape[1] // CORES
    core = lax.axis_index("core")
    own = lax.dynamic_slice_in_dim(weights, core * depth, depth, 1)
    two = exchange(own, 2)
    near = [exchange(own, 1), two]
    own, two = lax.optimization_barrier((own, two))
    near.append(lax.ppermute(own, "stage", [(1, 2), (2, 1)]))
    near.append(lax.ppermute(two, "stage", [(1, 0), (2, 3)]))
    far = [swap_cores(block) for block in near]
    spread = spread_blocks(adj_src, adj_blocks, halo_rows)
    arrived, spread, near, far = lax.optimization_barrier((arrived, spread, near, far))

    sums = halo_sums(arrived, spread, tiles)
    token, weights = lax.optimization_barrier((sums[0], weights))
    halos = exchange_all([token, *sums[1:]])
    group, own_x, own_a = stage_operands(weights, near, far, tiles, adj_blocks)

    *first, last = chain(0, own_x, own_a, group, halos)
    mirror = [(s, HALVES * STAGES - 1 - s) for s in range(STAGES)]
    done = chain(1, lax.ppermute(last, SEGMENT, mirror), own_a, group, halos, first)
    fresh = place(exchange_all(done))
    return fresh.reshape(1, rows_dev, width)


def solution(mesh):
    segments, parts = mesh.devices.shape
    devices = mesh.devices.reshape(HALVES, segments // HALVES, parts // CORES, CORES)
    fine = Mesh(devices, SEGMENT + DOM)
    placed = (
        P(DOM, None),
        P(SEGMENT, DOM, None),
        P(SEGMENT, None, None),
        P(DOM, None, None),
        P(DOM, None),
        P(DOM, None),
        P(DOM, None, None, None),
    )
    return jax.shard_map(
        local, mesh=fine, in_specs=placed, out_specs=P(SEGMENT, DOM, None), check_vma=False
    )
```

```python
import jax
import jax.numpy as jnp
import numpy as np
from jax import lax
from jax.experimental import pallas as pl
from jax.experimental.pallas import tpu as pltpu
from jax.sharding import Mesh, PartitionSpec as P

HALVES = 2
STAGES = 4
SLOTS = (0, 2, 3, 1)
CORES = 2
SEGMENT = ("half", "stage")
DOM = ("pair", "core")
ANYWHERE = pl.BlockSpec(memory_space=pl.ANY)
VMEM = pl.BlockSpec(memory_space=pltpu.VMEM)
GRANT = pltpu.CompilerParams(vmem_limit_bytes=60 * 1024 * 1024)
SMALL = pltpu.CompilerParams(vmem_limit_bytes=24 * 1024 * 1024)


def tile_of(slot):
    return lax.axis_index("stage") ^ (2 * lax.axis_index("half")) ^ slot


def exchange(block, slot):
    return lax.ppermute(block, "stage", [(u, u ^ slot) for u in range(STAGES)])


def exchange_all(blocks):
    return [block if slot == 0 else exchange(block, slot) for slot, block in zip(SLOTS, blocks)]


def swap_cores(block):
    return lax.ppermute(block, "core", [(0, 1), (1, 0)])


def spread_kernel(source_ref, blocks_ref, out_ref):
    tiles, picked, rows, _ = blocks_ref.shape
    out_ref[...] = jnp.zeros_like(out_ref)
    for t in range(tiles):
        for k in range(1, picked):
            first = pl.multiple_of((source_ref[t, k] - 1) * rows, rows)
            out_ref[t, :, pl.ds(first, rows)] = blocks_ref[t, k]


def spread_blocks(adj_src, adj_blocks, halo_rows):
    tiles, _, rows, _ = adj_blocks.shape
    return pl.pallas_call(
        spread_kernel,
        out_shape=jax.ShapeDtypeStruct((tiles, rows, halo_rows), jnp.bfloat16),
        in_specs=[pl.BlockSpec(memory_space=pltpu.SMEM), VMEM],
        out_specs=VMEM,
        compiler_params=GRANT,
    )(adj_src, adj_blocks)


def pick_kernel(rows_ref, count_ref, history_ref, out_ref, *scratch):
    history_buf, pick_buf, out_buf, in_sem, out_sem = scratch
    receivers, levels, slots, width = out_ref.shape
    rows = history_ref.shape[1]
    parts = in_sem.shape[1]
    some = rows // parts
    loads = [
        [
            pltpu.make_async_copy(
                history_ref.at[i, pl.ds(n * some, some)],
                history_buf.at[i, pl.ds(n * some, some)],
                in_sem.at[i, n],
            )
            for n in range(parts)
        ]
        for i in range(levels)
    ]
    for load in sum(loads, []):
        load.start()

    slot = lax.broadcasted_iota(jnp.int32, (slots, receivers), 0)
    wanted = jnp.where(slot < count_ref[...], rows_ref[0], -1)
    column = lax.broadcasted_iota(jnp.int32, (slots, rows), 1)
    for p in range(receivers):
        mask = jnp.where(wanted[:, p : p + 1] == column, 1.0, 0.0)
        pick_buf[p * slots : (p + 1) * slots] = mask.astype(jnp.bfloat16)

    chunks = out_sem.shape[1]
    group = receivers // chunks
    stores = []
    for i in range(levels):
        for load in loads[i]:
            load.wait()
        for n in range(chunks):
            got = jnp.dot(
                pick_buf[n * group * slots : (n + 1) * group * slots],
                history_buf[i],
                preferred_element_type=jnp.float32,
            )
            chosen = pl.ds(n * group, group)
            out_buf[i, chosen] = got.astype(jnp.bfloat16).reshape(group, slots, width)
            store = pltpu.make_async_copy(
                out_buf.at[i, chosen], out_ref.at[chosen, i], out_sem.at[i, n]
            )
            store.start()
            stores.append(store)
    for store in stores:
        store.wait()


def pick_rows(send_rows, send_count, history):
    parts, slots = send_rows.shape[1:]
    levels, rows, width = history.shape
    return pl.pallas_call(
        pick_kernel,
        out_shape=jax.ShapeDtypeStruct((parts, levels, slots, width), jnp.bfloat16),
        in_specs=[VMEM, VMEM, ANYWHERE],
        out_specs=ANYWHERE,
        scratch_shapes=[
            pltpu.VMEM(history.shape, jnp.bfloat16),
            pltpu.VMEM((parts * slots, rows), jnp.bfloat16),
            pltpu.VMEM((levels, parts, slots, width), jnp.bfloat16),
            pltpu.SemaphoreType.DMA((levels, 2)),
            pltpu.SemaphoreType.DMA((levels, 4)),
        ],
        compiler_params=GRANT,
        cost_estimate=pl.CostEstimate(
            flops=2 * levels * parts * slots * rows * width,
            bytes_accessed=2 * levels * (parts * slots + rows) * width,
            transcendentals=0,
        ),
    )(send_rows.swapaxes(1, 2), send_count, history)


def stage_kernel(*refs):
    shards = STAGES
    own_ref, near_refs, far_refs = refs[0], refs[1 : 1 + shards], refs[1 + shards : 1 + 2 * shards]
    features_ref, blocks_ref, group_ref, own_x_ref, own_a_ref, sem = refs[1 + 2 * shards :]
    depth = group_ref.shape[3]
    stage = lax.axis_index("stage")
    core = lax.axis_index("core")
    pairs = [
        (features_ref.at[tile_of(0)], own_x_ref),
        (blocks_ref.at[tile_of(0), 0], own_a_ref),
    ]
    for c in range(CORES):
        pairs.append((own_ref.at[:, pl.ds(c * depth, depth)], group_ref.at[stage, c]))
    for r in range(1, STAGES):
        pairs.append((near_refs[r - 1], group_ref.at[stage ^ r, core]))
        pairs.append((far_refs[r - 1], group_ref.at[stage ^ r, 1 - core]))
    copies = [pltpu.make_async_copy(*pair, sem.at[n]) for n, pair in enumerate(pairs)]
    late = len(copies) - 2
    inner = (stage == 1) | (stage == 2)
    for copy in copies[:late]:
        copy.start()

    @pl.when(inner)
    def _():
        for copy in copies[late:]:
            copy.start()

    @pl.when(jnp.logical_not(inner))
    def _():
        pltpu.make_async_copy(near_refs[-1], pairs[late][1], sem.at[late]).start()
        pltpu.make_async_copy(far_refs[-1], pairs[late + 1][1], sem.at[late + 1]).start()

    for copy in copies:
        copy.wait()


def stage_operands(weights, near, far, features, adj_blocks):
    levels, width, _ = weights.shape
    rows = adj_blocks.shape[2]
    sources = [weights, *near, *far, features, adj_blocks]
    shapes = [(STAGES, CORES, levels, width // CORES, width), (rows, width), (rows, rows)]
    return pl.pallas_call(
        stage_kernel,
        out_shape=[jax.ShapeDtypeStruct(shape, jnp.bfloat16) for shape in shapes],
        in_specs=[ANYWHERE] * len(sources),
        out_specs=[VMEM] * len(shapes),
        scratch_shapes=[pltpu.SemaphoreType.DMA((2 * STAGES + CORES,))],
        compiler_params=SMALL,
        cost_estimate=pl.CostEstimate(
            flops=0, bytes_accessed=4 * STAGES * weights.size, transcendentals=0
        ),
    )(*sources)


def halo_kernel(arrived_ref, spread_ref, features_ref, *refs):
    out_refs = refs[:STAGES]
    arrived_buf, spread_buf, features_buf, out_buf, in_sem, own_sem, out_sem = refs[STAGES:]
    parts, levels, slots, width = arrived_ref.shape
    rows = spread_ref.shape[1]
    own = []
    for n, r in enumerate(SLOTS):
        for m, (ref, buf) in enumerate([(spread_ref, spread_buf), (features_ref, features_buf)]):
            own.append(pltpu.make_async_copy(ref.at[tile_of(r)], buf.at[n], own_sem.at[m, n]))
    chunks = in_sem.shape[1]
    group = parts // chunks
    loads = [
        [
            pltpu.make_async_copy(
                arrived_ref.at[pl.ds(n * group, group), i],
                arrived_buf.at[i, pl.ds(n * group, group)],
                in_sem.at[i, n],
            )
            for n in range(chunks)
        ]
        for i in range(levels)
    ]
    for load in loads[0] + own + sum(loads[1:], []):
        load.start()
    for load in own:
        load.wait()
    spread = spread_buf[...].reshape(STAGES * rows, parts * slots)
    stores = []
    for i in range(levels):
        for load in loads[i]:
            load.wait()
        halo = arrived_buf[i].reshape(parts * slots, width)
        summed = jnp.dot(spread, halo, preferred_element_type=jnp.float32)
        for n in range(STAGES):
            start = 0.1 * features_buf[n].astype(jnp.float32)
            part = 0.9 * summed[n * rows : (n + 1) * rows] + start
            out_buf[n, i] = part.astype(jnp.bfloat16)
            store = pltpu.make_async_copy(out_buf.at[n, i], out_refs[n].at[i], out_sem.at[n, i])
            store.start()
            stores.append(store)
    for store in stores:
        store.wait()


def halo_sums(arrived, spread, features):
    parts, levels, slots, width = arrived.shape
    _, rows, halo_rows = spread.shape
    return pl.pallas_call(
        halo_kernel,
        out_shape=[jax.ShapeDtypeStruct((levels, rows, width), jnp.bfloat16)] * STAGES,
        in_specs=[ANYWHERE] * 3,
        out_specs=[ANYWHERE] * STAGES,
        scratch_shapes=[
            pltpu.VMEM((levels, parts, slots, width), jnp.bfloat16),
            pltpu.VMEM(spread.shape, jnp.bfloat16),
            pltpu.VMEM(features.shape, jnp.bfloat16),
            pltpu.VMEM((STAGES, levels, rows, width), jnp.bfloat16),
            pltpu.SemaphoreType.DMA((levels, 4)),
            pltpu.SemaphoreType.DMA((2, STAGES)),
            pltpu.SemaphoreType.DMA((STAGES, levels)),
        ],
        compiler_params=GRANT,
        cost_estimate=pl.CostEstimate(
            flops=2 * levels * STAGES * rows * halo_rows * width,
            bytes_accessed=2 * (arrived.size + spread.size + features.size * (1 + levels)),
            transcendentals=0,
        ),
    )(arrived, spread, features)


def chain_kernel(which, betas, x_ref, a_ref, w_ref, *refs):
    stages, cores, levels, depth, _ = w_ref.shape
    h_refs, refs = refs[:stages], refs[stages:]
    if which > 0:
        before_refs, refs = refs[:stages], refs[stages:]
    out_refs, h_buf = refs[:stages], refs[-1]
    half = lax.axis_index("half")
    stage = lax.axis_index("stage")

    @pl.when(half == which)
    def _():
        for r, h_ref in zip(SLOTS, h_refs):
            h_buf[stage ^ r] = h_ref[...]
        a = a_ref[...]
        x = x_ref[...]
        for s in range(stages):
            for i in range(levels):
                beta = betas[(which * stages + s) * levels + i]
                summed = jnp.dot(a, x, preferred_element_type=jnp.float32)
                support = 0.9 * summed + h_buf[s, i].astype(jnp.float32)
                rounded = support.astype(jnp.bfloat16)
                branch = sum(
                    jnp.dot(
                        rounded[:, c * depth : (c + 1) * depth],
                        w_ref[s, c, i],
                        preferred_element_type=jnp.float32,
                    )
                    for c in range(cores)
                )
                mixed = (1.0 - beta) * support + beta * branch
                x = jnp.maximum(mixed, 0.0).astype(jnp.bfloat16)
            for r, out_ref in zip(SLOTS, out_refs):

                @pl.when(stage ^ s == r)
                def _():
                    out_ref[...] = x

        if which == 0:
            refs[stages][...] = x

    if which > 0:

        @pl.when(half != which)
        def _():
            for r in range(stages):
                out_refs[r][...] = before_refs[r][...]


def chain(which, x, a, weights, halos, before=()):
    stages, _, levels, _, width = weights.shape
    rows = x.shape[0]
    order = np.arange(HALVES * stages * levels, dtype=np.float32)
    betas = [float(b) for b in np.log1p(np.float32(1.0) / (order + np.float32(1.0)))]
    outs = stages if before else stages + 1
    return pl.pallas_call(
        lambda *refs: chain_kernel(which, betas, *refs),
        out_shape=[jax.ShapeDtypeStruct((rows, width), jnp.bfloat16)] * outs,
        in_specs=[VMEM] * (3 + len(halos) + len(before)),
        out_specs=[VMEM] * outs,
        scratch_shapes=[pltpu.VMEM((stages, levels, rows, width), jnp.bfloat16)],
        compiler_params=SMALL,
        cost_estimate=pl.CostEstimate(
            flops=2 * stages * levels * rows * width * (width + rows),
            bytes_accessed=2 * stages * levels * width * (width + rows),
            transcendentals=0,
        ),
    )(x, a, weights, *halos, *before)


def place_kernel(*refs):
    in_refs, out_ref = refs[:-1], refs[-1]
    for r, ref in zip(SLOTS, in_refs):
        out_ref[0, tile_of(r)] = ref[...]


def place(tiles):
    rows, width = tiles[0].shape
    return pl.pallas_call(
        place_kernel,
        out_shape=jax.ShapeDtypeStruct((1, len(tiles), rows, width), jnp.bfloat16),
        in_specs=[VMEM] * len(tiles),
        out_specs=VMEM,
        compiler_params=SMALL,
    )(*tiles)


def local(features, history, weights, send_rows, send_count, adj_src, adj_blocks):
    rows_dev, width = features.shape
    tile_rows = adj_blocks.shape[2]
    parts, slots = send_rows.shape[1:]
    halo_rows = parts * slots
    tiles = features.reshape(STAGES, tile_rows, width)

    outgoing = pick_rows(send_rows, send_count, history)
    outgoing, adj_blocks, weights = lax.optimization_barrier((outgoing, adj_blocks, weights))
    arrived = lax.all_to_all(outgoing, DOM, split_axis=0, concat_axis=0, tiled=True)

    depth = weights.shape[1] // CORES
    core = lax.axis_index("core")
    own = lax.dynamic_slice_in_dim(weights, core * depth, depth, 1)
    two = exchange(own, 2)
    near = [exchange(own, 1), two]
    own, two = lax.optimization_barrier((own, two))
    near.append(lax.ppermute(own, "stage", [(1, 2), (2, 1)]))
    near.append(lax.ppermute(two, "stage", [(1, 0), (2, 3)]))
    far = [swap_cores(block) for block in near]
    spread = spread_blocks(adj_src, adj_blocks, halo_rows)
    arrived, spread, near, far = lax.optimization_barrier((arrived, spread, near, far))

    sums = halo_sums(arrived, spread, tiles)
    token, weights = lax.optimization_barrier((sums[0], weights))
    halos = exchange_all([token, *sums[1:]])
    group, own_x, own_a = stage_operands(weights, near, far, tiles, adj_blocks)

    *first, last = chain(0, own_x, own_a, group, halos)
    over = [(s, STAGES + (s ^ 2)) for s in range(STAGES)]
    done = chain(1, lax.ppermute(last, SEGMENT, over), own_a, group, halos, first)
    fresh = place(exchange_all(done))
    return fresh.reshape(1, rows_dev, width)


def solution(mesh):
    segments, parts = mesh.devices.shape
    devices = mesh.devices.reshape(HALVES, segments // HALVES, parts // CORES, CORES)
    fine = Mesh(devices, SEGMENT + DOM)
    placed = (
        P(DOM, None),
        P(SEGMENT, DOM, None),
        P(SEGMENT, None, None),
        P(DOM, None, None),
        P(DOM, None),
        P(DOM, None),
        P(DOM, None, None, None),
    )
    return jax.shard_map(
        local, mesh=fine, in_specs=placed, out_specs=P(SEGMENT, DOM, None), check_vma=False
    )
```

```python
import jax
import jax.numpy as jnp
import numpy as np
from jax import lax
from jax.experimental import pallas as pl
from jax.experimental.pallas import tpu as pltpu
from jax.sharding import Mesh, PartitionSpec as P

HALVES = 2
STAGES = 4
SLOTS = (0, 2, 3, 1)
CORES = 2
SEGMENT = ("half", "stage")
DOM = ("pair", "core")
ANYWHERE = pl.BlockSpec(memory_space=pl.ANY)
VMEM = pl.BlockSpec(memory_space=pltpu.VMEM)
GRANT = pltpu.CompilerParams(vmem_limit_bytes=60 * 1024 * 1024)
SMALL = pltpu.CompilerParams(vmem_limit_bytes=24 * 1024 * 1024)


def tile_of(slot):
    return lax.axis_index("stage") ^ (2 * lax.axis_index("half")) ^ slot


def exchange(block, slot):
    return lax.ppermute(block, "stage", [(u, u ^ slot) for u in range(STAGES)])


def exchange_all(blocks):
    return [block if slot == 0 else exchange(block, slot) for slot, block in zip(SLOTS, blocks)]


def swap_cores(block):
    return lax.ppermute(block, "core", [(0, 1), (1, 0)])


def spread_kernel(source_ref, blocks_ref, out_ref):
    tiles, picked, rows, _ = blocks_ref.shape
    out_ref[...] = jnp.zeros_like(out_ref)
    for t in range(tiles):
        for k in range(1, picked):
            first = pl.multiple_of((source_ref[t, k] - 1) * rows, rows)
            out_ref[t, :, pl.ds(first, rows)] = blocks_ref[t, k]


def spread_blocks(adj_src, adj_blocks, halo_rows):
    tiles, _, rows, _ = adj_blocks.shape
    return pl.pallas_call(
        spread_kernel,
        out_shape=jax.ShapeDtypeStruct((tiles, rows, halo_rows), jnp.bfloat16),
        in_specs=[pl.BlockSpec(memory_space=pltpu.SMEM), VMEM],
        out_specs=VMEM,
        compiler_params=GRANT,
    )(adj_src, adj_blocks)


def pick_kernel(rows_ref, count_ref, history_ref, out_ref, *scratch):
    rows_buf, count_buf, history_buf, pick_buf, out_buf, list_sem, in_sem, out_sem = scratch
    receivers, levels, slots, width = out_ref.shape
    rows = history_ref.shape[1]
    parts = in_sem.shape[1]
    some = rows // parts
    loads = [
        [
            pltpu.make_async_copy(
                history_ref.at[i, pl.ds(n * some, some)],
                history_buf.at[i, pl.ds(n * some, some)],
                in_sem.at[i, n],
            )
            for n in range(parts)
        ]
        for i in range(levels)
    ]
    lists = [
        pltpu.make_async_copy(rows_ref, rows_buf, list_sem.at[0]),
        pltpu.make_async_copy(count_ref, count_buf, list_sem.at[1]),
    ]
    for load in lists + sum(loads, []):
        load.start()
    for load in lists:
        load.wait()

    slot = lax.broadcasted_iota(jnp.int32, (slots, receivers), 0)
    wanted = jnp.where(slot < count_buf[...], rows_buf[0], -1)
    column = lax.broadcasted_iota(jnp.int32, (slots, rows), 1)
    for p in range(receivers):
        mask = jnp.where(wanted[:, p : p + 1] == column, 1.0, 0.0)
        pick_buf[p * slots : (p + 1) * slots] = mask.astype(jnp.bfloat16)

    chunks = out_sem.shape[1]
    group = receivers // chunks
    stores = []
    for i in range(levels):
        for load in loads[i]:
            load.wait()
        for n in range(chunks):
            got = jnp.dot(
                pick_buf[n * group * slots : (n + 1) * group * slots],
                history_buf[i],
                preferred_element_type=jnp.float32,
            )
            chosen = pl.ds(n * group, group)
            out_buf[i, chosen] = got.astype(jnp.bfloat16).reshape(group, slots, width)
            store = pltpu.make_async_copy(
                out_buf.at[i, chosen], out_ref.at[chosen, i], out_sem.at[i, n]
            )
            store.start()
            stores.append(store)
    for store in stores:
        store.wait()


def pick_rows(send_rows, send_count, history):
    parts, slots = send_rows.shape[1:]
    levels, rows, width = history.shape
    return pl.pallas_call(
        pick_kernel,
        out_shape=jax.ShapeDtypeStruct((parts, levels, slots, width), jnp.bfloat16),
        in_specs=[ANYWHERE] * 3,
        out_specs=ANYWHERE,
        scratch_shapes=[
            pltpu.VMEM((1, slots, parts), jnp.int32),
            pltpu.VMEM((1, parts), jnp.int32),
            pltpu.VMEM(history.shape, jnp.bfloat16),
            pltpu.VMEM((parts * slots, rows), jnp.bfloat16),
            pltpu.VMEM((levels, parts, slots, width), jnp.bfloat16),
            pltpu.SemaphoreType.DMA((2,)),
            pltpu.SemaphoreType.DMA((levels, 2)),
            pltpu.SemaphoreType.DMA((levels, 4)),
        ],
        compiler_params=GRANT,
        cost_estimate=pl.CostEstimate(
            flops=2 * levels * parts * slots * rows * width,
            bytes_accessed=2 * levels * (parts * slots + rows) * width,
            transcendentals=0,
        ),
    )(send_rows.swapaxes(1, 2), send_count, history)


def stage_kernel(*refs):
    shards = STAGES
    own_ref, near_refs, far_refs = refs[0], refs[1 : 1 + shards], refs[1 + shards : 1 + 2 * shards]
    features_ref, blocks_ref, group_ref, own_x_ref, own_a_ref, sem = refs[1 + 2 * shards :]
    depth = group_ref.shape[3]
    stage = lax.axis_index("stage")
    core = lax.axis_index("core")
    pairs = [
        (features_ref.at[tile_of(0)], own_x_ref),
        (blocks_ref.at[tile_of(0), 0], own_a_ref),
    ]
    for c in range(CORES):
        pairs.append((own_ref.at[:, pl.ds(c * depth, depth)], group_ref.at[stage, c]))
    for r in range(1, STAGES):
        pairs.append((near_refs[r - 1], group_ref.at[stage ^ r, core]))
        pairs.append((far_refs[r - 1], group_ref.at[stage ^ r, 1 - core]))
    copies = [pltpu.make_async_copy(*pair, sem.at[n]) for n, pair in enumerate(pairs)]
    late = len(copies) - 2
    inner = (stage == 1) | (stage == 2)
    for copy in copies[:late]:
        copy.start()

    @pl.when(inner)
    def _():
        for copy in copies[late:]:
            copy.start()

    @pl.when(jnp.logical_not(inner))
    def _():
        pltpu.make_async_copy(near_refs[-1], pairs[late][1], sem.at[late]).start()
        pltpu.make_async_copy(far_refs[-1], pairs[late + 1][1], sem.at[late + 1]).start()

    for copy in copies:
        copy.wait()


def stage_operands(weights, near, far, features, adj_blocks):
    levels, width, _ = weights.shape
    rows = adj_blocks.shape[2]
    sources = [weights, *near, *far, features, adj_blocks]
    shapes = [(STAGES, CORES, levels, width // CORES, width), (rows, width), (rows, rows)]
    return pl.pallas_call(
        stage_kernel,
        out_shape=[jax.ShapeDtypeStruct(shape, jnp.bfloat16) for shape in shapes],
        in_specs=[ANYWHERE] * len(sources),
        out_specs=[VMEM] * len(shapes),
        scratch_shapes=[pltpu.SemaphoreType.DMA((2 * STAGES + CORES,))],
        compiler_params=SMALL,
        cost_estimate=pl.CostEstimate(
            flops=0, bytes_accessed=4 * STAGES * weights.size, transcendentals=0
        ),
    )(*sources)


def halo_kernel(arrived_ref, spread_ref, *refs):
    out_refs = refs[:STAGES]
    arrived_buf, spread_buf, out_buf, in_sem, own_sem, out_sem = refs[STAGES:]
    parts, levels, slots, width = arrived_ref.shape
    rows = spread_ref.shape[1]
    spreads = [
        pltpu.make_async_copy(spread_ref.at[tile_of(r)], spread_buf.at[n], own_sem.at[n])
        for n, r in enumerate(SLOTS)
    ]
    chunks = in_sem.shape[1]
    group = parts // chunks
    loads = [
        [
            pltpu.make_async_copy(
                arrived_ref.at[pl.ds(n * group, group), i],
                arrived_buf.at[i, pl.ds(n * group, group)],
                in_sem.at[i, n],
            )
            for n in range(chunks)
        ]
        for i in range(levels)
    ]
    for load in spreads + sum(loads, []):
        load.start()
    for load in spreads + loads[0]:
        load.wait()
    stores = []
    for i in range(levels):
        if i > 0:
            for load in loads[i]:
                load.wait()
        summed = jnp.dot(
            spread_buf[...].reshape(STAGES * rows, parts * slots),
            arrived_buf[i].reshape(parts * slots, width),
            preferred_element_type=jnp.float32,
        )
        for n in range(STAGES):
            out_buf[n, i] = summed[n * rows : (n + 1) * rows].astype(jnp.bfloat16)
            store = pltpu.make_async_copy(out_buf.at[n, i], out_refs[n].at[i], out_sem.at[n, i])
            store.start()
            stores.append(store)
    for store in stores:
        store.wait()


def halo_sums(arrived, spread):
    parts, levels, slots, width = arrived.shape
    _, rows, halo_rows = spread.shape
    return pl.pallas_call(
        halo_kernel,
        out_shape=[jax.ShapeDtypeStruct((levels, rows, width), jnp.bfloat16)] * STAGES,
        in_specs=[ANYWHERE] * 2,
        out_specs=[ANYWHERE] * STAGES,
        scratch_shapes=[
            pltpu.VMEM((levels, parts, slots, width), jnp.bfloat16),
            pltpu.VMEM(spread.shape, jnp.bfloat16),
            pltpu.VMEM((STAGES, levels, rows, width), jnp.bfloat16),
            pltpu.SemaphoreType.DMA((levels, 4)),
            pltpu.SemaphoreType.DMA((STAGES,)),
            pltpu.SemaphoreType.DMA((STAGES, levels)),
        ],
        compiler_params=GRANT,
        cost_estimate=pl.CostEstimate(
            flops=2 * levels * STAGES * rows * halo_rows * width,
            bytes_accessed=2 * (arrived.size + spread.size + STAGES * levels * rows * width),
            transcendentals=0,
        ),
    )(arrived, spread)


def chain_kernel(which, betas, x_ref, features_ref, a_ref, w_ref, *refs):
    stages, cores, levels, depth, _ = w_ref.shape
    h_refs, refs = refs[:stages], refs[stages:]
    if which > 0:
        before_refs, refs = refs[:stages], refs[stages:]
    out_refs, h_buf = refs[:stages], refs[-1]
    half = lax.axis_index("half")
    stage = lax.axis_index("stage")

    @pl.when(half == which)
    def _():
        for r, h_ref in zip(SLOTS, h_refs):
            h_buf[stage ^ r] = h_ref[...]
        a = a_ref[...]
        x = x_ref[...]
        start = 0.1 * features_ref[...].astype(jnp.float32)
        for s in range(stages):
            for i in range(levels):
                beta = betas[(which * stages + s) * levels + i]
                summed = jnp.dot(a, x, preferred_element_type=jnp.float32)
                support = 0.9 * (summed + h_buf[s, i].astype(jnp.float32)) + start
                rounded = support.astype(jnp.bfloat16)
                branch = sum(
                    jnp.dot(
                        rounded[:, c * depth : (c + 1) * depth],
                        w_ref[s, c, i],
                        preferred_element_type=jnp.float32,
                    )
                    for c in range(cores)
                )
                mixed = (1.0 - beta) * support + beta * branch
                x = jnp.maximum(mixed, 0.0).astype(jnp.bfloat16)
            for r, out_ref in zip(SLOTS, out_refs):

                @pl.when(stage ^ s == r)
                def _():
                    out_ref[...] = x

        if which == 0:
            refs[stages][...] = x

    if which > 0:

        @pl.when(half != which)
        def _():
            for r in range(stages):
                out_refs[r][...] = before_refs[r][...]


def chain(which, x, features, a, weights, halos, before=()):
    stages, _, levels, _, width = weights.shape
    rows = x.shape[0]
    order = np.arange(HALVES * stages * levels, dtype=np.float32)
    betas = [float(b) for b in np.log1p(np.float32(1.0) / (order + np.float32(1.0)))]
    outs = stages if before else stages + 1
    return pl.pallas_call(
        lambda *refs: chain_kernel(which, betas, *refs),
        out_shape=[jax.ShapeDtypeStruct((rows, width), jnp.bfloat16)] * outs,
        in_specs=[VMEM] * (4 + len(halos) + len(before)),
        out_specs=[VMEM] * outs,
        scratch_shapes=[pltpu.VMEM((stages, levels, rows, width), jnp.bfloat16)],
        compiler_params=SMALL,
        cost_estimate=pl.CostEstimate(
            flops=2 * stages * levels * rows * width * (width + rows),
            bytes_accessed=2 * stages * levels * width * (width + rows),
            transcendentals=0,
        ),
    )(x, features, a, weights, *halos, *before)


def place_kernel(*refs):
    in_refs, out_ref = refs[:-1], refs[-1]
    for r, ref in zip(SLOTS, in_refs):
        out_ref[0, tile_of(r)] = ref[...]


def place(tiles):
    rows, width = tiles[0].shape
    return pl.pallas_call(
        place_kernel,
        out_shape=jax.ShapeDtypeStruct((1, len(tiles), rows, width), jnp.bfloat16),
        in_specs=[VMEM] * len(tiles),
        out_specs=VMEM,
        compiler_params=SMALL,
    )(*tiles)


def local(features, history, weights, send_rows, send_count, adj_src, adj_blocks):
    rows_dev, width = features.shape
    tile_rows = adj_blocks.shape[2]
    parts, slots = send_rows.shape[1:]
    halo_rows = parts * slots
    tiles = features.reshape(STAGES, tile_rows, width)

    outgoing = pick_rows(send_rows, send_count, history)
    outgoing, adj_blocks, weights = lax.optimization_barrier((outgoing, adj_blocks, weights))
    arrived = lax.all_to_all(outgoing, DOM, split_axis=0, concat_axis=0, tiled=True)

    depth = weights.shape[1] // CORES
    core = lax.axis_index("core")
    own = lax.dynamic_slice_in_dim(weights, core * depth, depth, 1)
    two = exchange(own, 2)
    near = [exchange(own, 1), two]
    own, two = lax.optimization_barrier((own, two))
    near.append(lax.ppermute(own, "stage", [(1, 2), (2, 1)]))
    near.append(lax.ppermute(two, "stage", [(1, 0), (2, 3)]))
    far = [swap_cores(block) for block in near]
    spread = spread_blocks(adj_src, adj_blocks, halo_rows)
    arrived, spread, near, far = lax.optimization_barrier((arrived, spread, near, far))

    sums = halo_sums(arrived, spread)
    token, weights = lax.optimization_barrier((sums[0], weights))
    halos = exchange_all([token, *sums[1:]])
    group, own_x, own_a = stage_operands(weights, near, far, tiles, adj_blocks)

    *first, last = chain(0, own_x, own_x, own_a, group, halos)
    over = [(s, STAGES + (s ^ 2)) for s in range(STAGES)]
    done = chain(1, lax.ppermute(last, SEGMENT, over), own_x, own_a, group, halos, first)
    fresh = place(exchange_all(done))
    return fresh.reshape(1, rows_dev, width)


def solution(mesh):
    segments, parts = mesh.devices.shape
    devices = mesh.devices.reshape(HALVES, segments // HALVES, parts // CORES, CORES)
    fine = Mesh(devices, SEGMENT + DOM)
    placed = (
        P(DOM, None),
        P(SEGMENT, DOM, None),
        P(SEGMENT, None, None),
        P(DOM, None, None),
        P(DOM, None),
        P(DOM, None),
        P(DOM, None, None, None),
    )
    return jax.shard_map(
        local, mesh=fine, in_specs=placed, out_specs=P(SEGMENT, DOM, None), check_vma=False
    )
```

```python
import jax
import jax.numpy as jnp
import numpy as np
from jax import lax
from jax.experimental import pallas as pl
from jax.experimental.pallas import tpu as pltpu
from jax.sharding import Mesh, PartitionSpec as P

HALVES = 2
STAGES = 4
SLOTS = (0, 2, 3, 1)
CORES = 2
SEGMENT = ("half", "stage")
DOM = ("pair", "core")
ANYWHERE = pl.BlockSpec(memory_space=pl.ANY)
VMEM = pl.BlockSpec(memory_space=pltpu.VMEM)
GRANT = pltpu.CompilerParams(vmem_limit_bytes=60 * 1024 * 1024)
SMALL = pltpu.CompilerParams(vmem_limit_bytes=24 * 1024 * 1024)


def tile_of(slot):
    return lax.axis_index("stage") ^ (2 * lax.axis_index("half")) ^ slot


def exchange(block, slot):
    return lax.ppermute(block, "stage", [(u, u ^ slot) for u in range(STAGES)])


def exchange_all(blocks):
    return [block if slot == 0 else exchange(block, slot) for slot, block in zip(SLOTS, blocks)]


def swap_cores(block):
    return lax.ppermute(block, "core", [(0, 1), (1, 0)])


def spread_kernel(source_ref, blocks_ref, out_ref):
    tiles, picked, rows, _ = blocks_ref.shape
    out_ref[...] = jnp.zeros_like(out_ref)
    for t in range(tiles):
        for k in range(1, picked):
            first = pl.multiple_of((source_ref[t, k] - 1) * rows, rows)
            out_ref[t, :, pl.ds(first, rows)] = blocks_ref[t, k]


def spread_blocks(adj_src, adj_blocks, halo_rows):
    tiles, _, rows, _ = adj_blocks.shape
    return pl.pallas_call(
        spread_kernel,
        out_shape=jax.ShapeDtypeStruct((tiles, rows, halo_rows), jnp.bfloat16),
        in_specs=[pl.BlockSpec(memory_space=pltpu.SMEM), VMEM],
        out_specs=VMEM,
        compiler_params=GRANT,
    )(adj_src, adj_blocks)


def pick_kernel(rows_ref, count_ref, history_ref, out_ref, *scratch):
    rows_buf, count_buf, history_buf, pick_buf, out_buf, list_sem, in_sem, out_sem = scratch
    receivers, levels, slots, width = out_ref.shape
    rows = history_ref.shape[1]
    parts = in_sem.shape[1]
    some = rows // parts
    loads = [
        [
            pltpu.make_async_copy(
                history_ref.at[i, pl.ds(n * some, some)],
                history_buf.at[i, pl.ds(n * some, some)],
                in_sem.at[i, n],
            )
            for n in range(parts)
        ]
        for i in range(levels)
    ]
    lists = [
        pltpu.make_async_copy(rows_ref, rows_buf, list_sem.at[0]),
        pltpu.make_async_copy(count_ref, count_buf, list_sem.at[1]),
    ]
    for load in lists + sum(loads, []):
        load.start()
    for load in lists:
        load.wait()

    slot = lax.broadcasted_iota(jnp.int32, (slots, receivers), 0)
    wanted = jnp.where(slot < count_buf[...], rows_buf[0], -1)
    column = lax.broadcasted_iota(jnp.int32, (slots, rows), 1)
    for p in range(receivers):
        mask = jnp.where(wanted[:, p : p + 1] == column, 1.0, 0.0)
        pick_buf[p * slots : (p + 1) * slots] = mask.astype(jnp.bfloat16)

    chunks = out_sem.shape[1]
    group = receivers // chunks
    stores = []
    for i in range(levels):
        for load in loads[i]:
            load.wait()
        for n in range(chunks):
            got = jnp.dot(
                pick_buf[n * group * slots : (n + 1) * group * slots],
                history_buf[i],
                preferred_element_type=jnp.float32,
            )
            chosen = pl.ds(n * group, group)
            out_buf[i, chosen] = got.astype(jnp.bfloat16).reshape(group, slots, width)
            store = pltpu.make_async_copy(
                out_buf.at[i, chosen], out_ref.at[chosen, i], out_sem.at[i, n]
            )
            store.start()
            stores.append(store)
    for store in stores:
        store.wait()


def pick_rows(send_rows, send_count, history):
    parts, slots = send_rows.shape[1:]
    levels, rows, width = history.shape
    return pl.pallas_call(
        pick_kernel,
        out_shape=jax.ShapeDtypeStruct((parts, levels, slots, width), jnp.bfloat16),
        in_specs=[ANYWHERE] * 3,
        out_specs=ANYWHERE,
        scratch_shapes=[
            pltpu.VMEM((1, slots, parts), jnp.int32),
            pltpu.VMEM((1, parts), jnp.int32),
            pltpu.VMEM(history.shape, jnp.bfloat16),
            pltpu.VMEM((parts * slots, rows), jnp.bfloat16),
            pltpu.VMEM((levels, parts, slots, width), jnp.bfloat16),
            pltpu.SemaphoreType.DMA((2,)),
            pltpu.SemaphoreType.DMA((levels, 2)),
            pltpu.SemaphoreType.DMA((levels, 4)),
        ],
        compiler_params=GRANT,
        cost_estimate=pl.CostEstimate(
            flops=2 * levels * parts * slots * rows * width,
            bytes_accessed=2 * levels * (parts * slots + rows) * width,
            transcendentals=0,
        ),
    )(send_rows.swapaxes(1, 2), send_count, history)


def stage_kernel(*refs):
    own_ref, near_refs, far_refs = refs[0], refs[1:STAGES], refs[STAGES : 2 * STAGES - 1]
    features_ref, blocks_ref, group_ref, own_x_ref, own_a_ref, sem = refs[2 * STAGES - 1 :]
    depth = group_ref.shape[3]
    stage = lax.axis_index("stage")
    core = lax.axis_index("core")
    pairs = [
        (features_ref.at[tile_of(0)], own_x_ref),
        (blocks_ref.at[tile_of(0), 0], own_a_ref),
    ]
    for c in range(CORES):
        pairs.append((own_ref.at[:, pl.ds(c * depth, depth)], group_ref.at[stage, c]))
    for r in range(1, STAGES):
        pairs.append((near_refs[r - 1], group_ref.at[stage ^ r, core]))
        pairs.append((far_refs[r - 1], group_ref.at[stage ^ r, 1 - core]))
    copies = [pltpu.make_async_copy(*pair, sem.at[n]) for n, pair in enumerate(pairs)]
    for copy in copies:
        copy.start()
    for copy in copies:
        copy.wait()


def stage_operands(weights, near, far, features, adj_blocks):
    levels, width, _ = weights.shape
    rows = adj_blocks.shape[2]
    sources = [weights, *near, *far, features, adj_blocks]
    shapes = [(STAGES, CORES, levels, width // CORES, width), (rows, width), (rows, rows)]
    return pl.pallas_call(
        stage_kernel,
        out_shape=[jax.ShapeDtypeStruct(shape, jnp.bfloat16) for shape in shapes],
        in_specs=[ANYWHERE] * len(sources),
        out_specs=[VMEM] * len(shapes),
        scratch_shapes=[pltpu.SemaphoreType.DMA((2 * STAGES + CORES,))],
        compiler_params=SMALL,
        cost_estimate=pl.CostEstimate(
            flops=0, bytes_accessed=4 * STAGES * weights.size, transcendentals=0
        ),
    )(*sources)


def halo_kernel(arrived_ref, spread_ref, *refs):
    out_refs = refs[:STAGES]
    arrived_buf, spread_buf, out_buf, in_sem, own_sem, out_sem = refs[STAGES:]
    parts, levels, slots, width = arrived_ref.shape
    rows = spread_ref.shape[1]
    spreads = [
        pltpu.make_async_copy(spread_ref.at[tile_of(r)], spread_buf.at[n], own_sem.at[n])
        for n, r in enumerate(SLOTS)
    ]
    chunks = in_sem.shape[1]
    group = parts // chunks
    loads = [
        [
            pltpu.make_async_copy(
                arrived_ref.at[pl.ds(n * group, group), i],
                arrived_buf.at[i, pl.ds(n * group, group)],
                in_sem.at[i, n],
            )
            for n in range(chunks)
        ]
        for i in range(levels)
    ]
    for load in spreads + sum(loads, []):
        load.start()
    for load in spreads + loads[0]:
        load.wait()
    stores = []
    for i in range(levels):
        if i > 0:
            for load in loads[i]:
                load.wait()
        summed = jnp.dot(
            spread_buf[...].reshape(STAGES * rows, parts * slots),
            arrived_buf[i].reshape(parts * slots, width),
            preferred_element_type=jnp.float32,
        )
        for n in range(STAGES):
            out_buf[n, i] = summed[n * rows : (n + 1) * rows].astype(jnp.bfloat16)
            store = pltpu.make_async_copy(out_buf.at[n, i], out_refs[n].at[i], out_sem.at[n, i])
            store.start()
            stores.append(store)
    for store in stores:
        store.wait()


def halo_sums(arrived, spread):
    parts, levels, slots, width = arrived.shape
    _, rows, halo_rows = spread.shape
    return pl.pallas_call(
        halo_kernel,
        out_shape=[jax.ShapeDtypeStruct((levels, rows, width), jnp.bfloat16)] * STAGES,
        in_specs=[ANYWHERE] * 2,
        out_specs=[ANYWHERE] * STAGES,
        scratch_shapes=[
            pltpu.VMEM((levels, parts, slots, width), jnp.bfloat16),
            pltpu.VMEM(spread.shape, jnp.bfloat16),
            pltpu.VMEM((STAGES, levels, rows, width), jnp.bfloat16),
            pltpu.SemaphoreType.DMA((levels, 4)),
            pltpu.SemaphoreType.DMA((STAGES,)),
            pltpu.SemaphoreType.DMA((STAGES, levels)),
        ],
        compiler_params=GRANT,
        cost_estimate=pl.CostEstimate(
            flops=2 * levels * STAGES * rows * halo_rows * width,
            bytes_accessed=2 * (arrived.size + spread.size + STAGES * levels * rows * width),
            transcendentals=0,
        ),
    )(arrived, spread)


def chain_kernel(which, betas, x_ref, features_ref, a_ref, w_ref, *refs):
    stages, cores, levels, depth, _ = w_ref.shape
    h_refs, refs = refs[:stages], refs[stages:]
    if which > 0:
        before_refs, refs = refs[:stages], refs[stages:]
    out_refs, h_buf = refs[:stages], refs[-1]
    half = lax.axis_index("half")
    stage = lax.axis_index("stage")

    @pl.when(half == which)
    def _():
        for r, h_ref in zip(SLOTS, h_refs):
            h_buf[stage ^ r] = h_ref[...]
        a = a_ref[...]
        x = x_ref[...]
        start = 0.1 * features_ref[...].astype(jnp.float32)
        for s in range(stages):
            for i in range(levels):
                beta = betas[(which * stages + s) * levels + i]
                summed = jnp.dot(a, x, preferred_element_type=jnp.float32)
                support = 0.9 * (summed + h_buf[s, i].astype(jnp.float32)) + start
                rounded = support.astype(jnp.bfloat16)
                branch = sum(
                    jnp.dot(
                        rounded[:, c * depth : (c + 1) * depth],
                        w_ref[s, c, i],
                        preferred_element_type=jnp.float32,
                    )
                    for c in range(cores)
                )
                mixed = (1.0 - beta) * support + beta * branch
                x = jnp.maximum(mixed, 0.0).astype(jnp.bfloat16)
            for r, out_ref in zip(SLOTS, out_refs):

                @pl.when(stage ^ s == r)
                def _():
                    out_ref[...] = x

        if which == 0:
            refs[stages][...] = x

    if which > 0:

        @pl.when(half != which)
        def _():
            for r in range(stages):
                out_refs[r][...] = before_refs[r][...]


def chain(which, x, features, a, weights, halos, before=()):
    stages, _, levels, _, width = weights.shape
    rows = x.shape[0]
    order = np.arange(HALVES * stages * levels, dtype=np.float32)
    betas = [float(b) for b in np.log1p(np.float32(1.0) / (order + np.float32(1.0)))]
    outs = stages if before else stages + 1
    return pl.pallas_call(
        lambda *refs: chain_kernel(which, betas, *refs),
        out_shape=[jax.ShapeDtypeStruct((rows, width), jnp.bfloat16)] * outs,
        in_specs=[VMEM] * (4 + len(halos) + len(before)),
        out_specs=[VMEM] * outs,
        scratch_shapes=[pltpu.VMEM((stages, levels, rows, width), jnp.bfloat16)],
        compiler_params=SMALL,
        cost_estimate=pl.CostEstimate(
            flops=2 * stages * levels * rows * width * (width + rows),
            bytes_accessed=2 * stages * levels * width * (width + rows),
            transcendentals=0,
        ),
    )(x, features, a, weights, *halos, *before)


def place_kernel(*refs):
    in_refs, out_ref = refs[:-1], refs[-1]
    for r, ref in zip(SLOTS, in_refs):
        out_ref[0, tile_of(r)] = ref[...]


def place(tiles):
    rows, width = tiles[0].shape
    return pl.pallas_call(
        place_kernel,
        out_shape=jax.ShapeDtypeStruct((1, len(tiles), rows, width), jnp.bfloat16),
        in_specs=[VMEM] * len(tiles),
        out_specs=VMEM,
        compiler_params=SMALL,
    )(*tiles)


def local(features, history, weights, send_rows, send_count, adj_src, adj_blocks):
    rows_dev, width = features.shape
    tile_rows = adj_blocks.shape[2]
    parts, slots = send_rows.shape[1:]
    halo_rows = parts * slots
    tiles = features.reshape(STAGES, tile_rows, width)

    outgoing = pick_rows(send_rows, send_count, history)
    outgoing, adj_blocks, weights = lax.optimization_barrier((outgoing, adj_blocks, weights))
    arrived = lax.all_to_all(outgoing, DOM, split_axis=0, concat_axis=0, tiled=True)

    depth = weights.shape[1] // CORES
    core = lax.axis_index("core")
    own = lax.dynamic_slice_in_dim(weights, core * depth, depth, 1)
    two = exchange(own, 2)
    near = [exchange(own, 1), two]
    near.append(exchange(two, 1))
    far = [swap_cores(block) for block in near]
    spread = spread_blocks(adj_src, adj_blocks, halo_rows)
    arrived, spread, near, far = lax.optimization_barrier((arrived, spread, near, far))

    sums = halo_sums(arrived, spread)
    token, weights = lax.optimization_barrier((sums[0], weights))
    halos = exchange_all([token, *sums[1:]])
    group, own_x, own_a = stage_operands(weights, near, far, tiles, adj_blocks)

    *first, last = chain(0, own_x, own_x, own_a, group, halos)
    over = [(s, STAGES + (s ^ 2)) for s in range(STAGES)]
    done = chain(1, lax.ppermute(last, SEGMENT, over), own_x, own_a, group, halos, first)
    fresh = place(exchange_all(done))
    return fresh.reshape(1, rows_dev, width)


def solution(mesh):
    segments, parts = mesh.devices.shape
    devices = mesh.devices.reshape(HALVES, segments // HALVES, parts // CORES, CORES)
    fine = Mesh(devices, SEGMENT + DOM)
    placed = (
        P(DOM, None),
        P(SEGMENT, DOM, None),
        P(SEGMENT, None, None),
        P(DOM, None, None),
        P(DOM, None),
        P(DOM, None),
        P(DOM, None, None, None),
    )
    return jax.shard_map(
        local, mesh=fine, in_specs=placed, out_specs=P(SEGMENT, DOM, None), check_vma=False
    )
```
